128 devices in a mesh: row: 16 (over x, y_lo, core), col: 8 (over z, y_hi).
Axes of the slice: x: 4, y: 4 (y_hi: 2, y_lo: 2; y = y_hi * 2 + y_lo), z: 4, core: 2. Of those that a mesh axis runs over, the one named last changes fastest.
Arguments:
- orbitals: bfloat16 [12288, 6144], P('col', 'row'), may hold values from -6 to 6
- fock_blocks: bfloat16 [65536, 1024], P(('row', 'col')), may hold values from -0.078125 to 0.078125
- fock_where: int32 [65536], P(('row', 'col')), may hold values from 0 to 1151, as said below
- density_blocks: bfloat16 [5120, 1024], P(('row', 'col')), may hold values from -6 to 6
- integrals: bfloat16 [1024, 1024, 1024], P(('row', 'col')), may hold values from -0.1875 to 0.1875
- quartet_density: int32 [1024], P(('row', 'col')), may hold values from 0 to 5119, as said below
- quartet_target: int32 [1024], P(('row', 'col')), may hold values from 0 to 4095, as said below
- quartet_count: int32 [128], P(('row', 'col')), may hold values from 1 to 8, as said below
Outputs:
- applied_fock: bfloat16 [12288, 6144], P('row', 'col')
The draws below stay inside these ranges and needn't reach their ends.
Inputs may be any that keep to these rules, and one draw needn't show every extreme that they name: `fock_where`: within one device the positions are distinct, from 0 to 1151. `quartet_density`: A quartet held by a device in row r names a density block held by a device in row r - 1, r or r + 1 (cyclically over 16 rows); device d holds blocks d * 40 to d * 40 + 39. `quartet_target`: the value t names block t % 512 of the device in column t // 512 of the quartet's own row. `quartet_count`: some device holds 8 live quartets; live quartets are the first slots of a device.
All inputs are finite; a program needn't handle non-finite values.
Results may differ from the reference program's by a relative error of at most 0.02.
Values may be sent and summed in bfloat16 or wider, within the bound.
No kernel may reach another device: no remote copies, remote signals or barrier semaphores. Data moves between devices by JAX's collectives and lax.ppermute only.
A program may use at most 320 MiB of HBM per device.

```python
import jax
import jax.numpy as jnp
from jax import lax

BS = 32
NA = 12288
NORB = 6144
KCAP = 512
PCAP = 40
QCAP = 8
TROWS = 24
TCOLS = 48
TILE = 1152
FOCKS = 65536
DENSITIES = 5120
QUARTETS = 1024
N_ROW = 16
N_COL = 8


def draw_fock_where(key, part):
    key = jax.random.fold_in(key, 12)
    keys = jax.random.split(key, N_ROW * N_COL)

    def one_device(device_key):
        return jax.random.permutation(device_key, TILE)[:KCAP].astype(jnp.int32)
    return jax.vmap(one_device)(keys).reshape(-1)


def draw_quartet_density(key, part):
    key = jax.random.fold_in(key, 13)
    first_key, second_key, third_key = jax.random.split(key, 3)
    total = N_ROW * N_COL * QCAP
    owner_row = jnp.arange(total, dtype=jnp.int32) // QCAP // N_COL
    offset = jax.random.randint(first_key, (total,), -1, 2, dtype=jnp.int32)
    source_row = (owner_row + offset + N_ROW) % N_ROW
    source_col = jax.random.randint(second_key, (total,), 0, N_COL, dtype=jnp.int32)
    slot_index = jax.random.randint(third_key, (total,), 0, PCAP, dtype=jnp.int32)
    return ((source_row * N_COL + source_col) * PCAP + slot_index).astype(jnp.int32)


def draw_quartet_target(key, part):
    key = jax.random.fold_in(key, 14)
    first_key, second_key = jax.random.split(key, 2)
    total = N_ROW * N_COL * QCAP
    target_col = jax.random.randint(first_key, (total,), 0, N_COL, dtype=jnp.int32)
    slot_index = jax.random.randint(second_key, (total,), 0, KCAP, dtype=jnp.int32)
    return (target_col * KCAP + slot_index).astype(jnp.int32)


def draw_quartet_count(key, part):
    key = jax.random.fold_in(key, 15)
    first_key, second_key, third_key = jax.random.split(key, 3)
    devices_total = N_ROW * N_COL
    first_draw = jax.random.randint(first_key, (devices_total,), 1, QCAP + 1, dtype=jnp.int32)
    second_draw = jax.random.randint(second_key, (devices_total,), 1, QCAP + 1, dtype=jnp.int32)
    smaller = jnp.minimum(first_draw, second_draw)
    busiest = jax.random.randint(third_key, (), 0, devices_total, dtype=jnp.int32)
    return jnp.where(jnp.arange(devices_total, dtype=jnp.int32) == busiest, QCAP, smaller).astype(jnp.int32)


def level_of(own_key, dims, pieces, smallest, top_value):
    level, own = 1.0, jax.random.fold_in(own_key, 6)
    for axis_at, blocks in pieces:
        draws = jnp.exp(jax.random.uniform(jax.random.fold_in(own, axis_at), (blocks,), jnp.float32, smallest / len(pieces), top_value / len(pieces)))
        level = level * jnp.repeat(draws, dims[axis_at] // blocks).reshape([-1 if axis == axis_at else 1 for axis in range(len(dims))])
    return level


def noise(rng, extent, scale, bound, cuts=(), kind=jnp.bfloat16):
    array = scale * jax.random.normal(rng, extent, jnp.float32)
    if cuts:
        array = array * level_of(rng, extent, cuts, -0.22, 0.18)
    return jnp.clip(array, -bound, bound).astype(kind)


def setup_inputs(seed: int = 0) -> dict:
    key_list = jax.random.split(jax.random.key(seed), 9)
    orbitals = noise(key_list[0], (NA, NORB), 1.0, 6.0, ((0, 8), (1, 16)))
    fock_blocks = noise(key_list[1], (FOCKS, BS * BS), (N_ROW * N_COL * KCAP * BS * BS // NA) ** -0.5, 0.078125, ((0, 128),))
    fock_where = draw_fock_where(jax.random.fold_in(key_list[8], 71), 0)
    density_blocks = noise(key_list[3], (DENSITIES, BS * BS), 1.0, 6.0, ((0, 128),))
    integrals = noise(key_list[4], (QUARTETS, BS * BS, BS * BS), (BS * BS) ** -0.5, 0.1875, ((0, 128),))
    quartet_density = draw_quartet_density(jax.random.fold_in(key_list[8], 71), 0)
    quartet_target = draw_quartet_target(jax.random.fold_in(key_list[8], 71), 0)
    quartet_count = draw_quartet_count(jax.random.fold_in(key_list[8], 71), 0)
    return {"orbitals": orbitals, "fock_blocks": fock_blocks, "fock_where": fock_where, "density_blocks": density_blocks, "integrals": integrals, "quartet_density": quartet_density, "quartet_target": quartet_target, "quartet_count": quartet_count}


def reference(orbitals, fock_blocks, fock_where, density_blocks, integrals, quartet_density, quartet_target, quartet_count):
    device_count = N_ROW * N_COL
    quartet_total = device_count * QCAP

    def contract(entry_pair):
        matrix, block_index = entry_pair
        return jnp.dot(matrix, density_blocks[block_index], preferred_element_type=jnp.float32)

    exchange_terms = lax.map(contract, (integrals, quartet_density))
    slot_ids = jnp.arange(quartet_total, dtype=jnp.int32)
    owner_device = slot_ids // QCAP
    alive_mask = (slot_ids % QCAP) < quartet_count[owner_device]
    exchange_terms = jnp.where(alive_mask[:, None], exchange_terms, jnp.zeros_like(exchange_terms))
    target = (owner_device // N_COL) * (N_COL * KCAP) + quartet_target
    update = jax.ops.segment_sum(exchange_terms, target, num_segments=device_count * KCAP)
    fock_new = (fock_blocks.astype(jnp.float32) + 0.25 * update).astype(jnp.bfloat16)
    fock_new = fock_new.reshape(N_ROW, N_COL, KCAP, BS * BS)
    places = fock_where.reshape(N_ROW, N_COL, KCAP)
    columns = orbitals.reshape(N_COL, TCOLS * BS, NORB)

    def one_row(row_inputs):
        blocks_row, places_row = row_inputs

        def one_tile(running, tile_inputs):
            blocks, spots, orbital_part = tile_inputs
            fock_tile = jnp.zeros((TILE, BS * BS), blocks.dtype).at[spots].set(blocks)
            fock_tile = fock_tile.reshape(TROWS, TCOLS, BS, BS).transpose(0, 2, 1, 3).reshape(TROWS * BS, TCOLS * BS)
            partial_value = jnp.dot(fock_tile, orbital_part, preferred_element_type=jnp.float32).astype(jnp.bfloat16)
            return running + partial_value.astype(jnp.float32), None

        row_total, unused = lax.scan(one_tile, jnp.zeros((TROWS * BS, NORB), jnp.float32), (blocks_row, places_row, columns))
        return row_total.astype(jnp.bfloat16)

    row_results = lax.map(one_row, (fock_new, places))
    return row_results.reshape(NA, NORB)
```

```python
import functools

import jax
import jax.numpy as jnp
import numpy as np
from jax import lax
from jax.experimental import pallas as pl
from jax.experimental.pallas import tpu as pltpu
from jax.sharding import PartitionSpec as P

BS = 32
TROWS, TCOLS = 24, 48
KCAP, PCAP, QCAP = 512, 40, 8
ROWS, COLS = TROWS * BS, TCOLS * BS
GROUPS = TCOLS // 4
EXT = 1024 + 128
W = 128
AXES = ("row", "col")
MB = 1 << 20
bf16, f32 = jnp.bfloat16, jnp.float32


def coords(d):
    r, k = d // 8, d % 8
    return dict(x=r // 4, yl=r // 2 % 2, c=r % 2, z=k // 2, yh=k % 2)


def number(x, yl, c, z, yh):
    return ((x % 4) * 4 + yl * 2 + c) * 8 + (z % 4) * 2 + yh


def move(value, to):
    pairs = []
    for d in range(128):
        place = coords(d)
        target = dict(place)
        target.update(to(**place))
        pairs.append((d, number(**target)))
    return lax.ppermute(value, AXES, pairs)


def shift_x(value, by):
    return move(value, lambda x, **o: dict(x=x + by))


def shift_z(value, by):
    return move(value, lambda z, **o: dict(z=z + by))


def swap_core(value):
    return move(value, lambda c, **o: dict(c=1 - c))


def swap_yh(value):
    return move(value, lambda yh, **o: dict(yh=1 - yh))


def shift_row(value, by):
    pairs = [(d, (d + 8 * by) % 128) for d in range(128)]
    return lax.ppermute(value, AXES, pairs)


def move_y(value, table):
    def to(yl, yh, **o):
        y = table[yh * 2 + yl]
        return dict(yl=y % 2, yh=y // 2)

    return move(value, to)


def here():
    r, k = lax.axis_index("row"), lax.axis_index("col")
    return dict(r=r, k=k, x=r // 4, yl=r // 2 % 2, c=r % 2, z=k // 2, yh=k % 2)


def call(kernel, out_shape, flops, nbytes, **kw):
    return pl.pallas_call(
        kernel,
        out_shape=out_shape,
        compiler_params=pltpu.CompilerParams(vmem_limit_bytes=56 * MB),
        cost_estimate=pl.CostEstimate(flops=flops, bytes_accessed=nbytes, transcendentals=0),
        **kw,
    )


VM = pl.BlockSpec(memory_space=pltpu.VMEM)
SM = pl.BlockSpec(memory_space=pltpu.SMEM)
ANY = pl.BlockSpec(memory_space=pl.ANY)


def select_kernel(req_own, req_a, req_b, p0, p1, p2, p3, out_own, out_a, out_b):
    at = here()
    parts = (p0, p1, p2, p3)
    steps = (0, 3, 1, 2)
    span = 2 * PCAP
    lane = lax.broadcasted_iota(jnp.int32, (16, span), 1)
    row = lax.broadcasted_iota(jnp.int32, (16, span), 0)
    for req, out in ((req_own, out_own), (req_a, out_a), (req_b, out_b)):
        want = jnp.full((16, span), -1, jnp.int32)
        for q in range(QCAP):
            want = jnp.where(row == q, req[q], want)
        total = jnp.zeros((16, 1024), f32)
        for part, step in zip(parts, steps):
            z = (at["z"] + step) % 4
            yh = jnp.where(lane < PCAP, at["yh"], 1 - at["yh"])
            held = (at["r"] * 8 + z * 2 + yh) * PCAP + jnp.where(lane < PCAP, lane, lane - PCAP)
            hot = (want == held).astype(f32).astype(bf16)
            total = total + jnp.dot(hot, part[...], preferred_element_type=f32)
        out[...] = total.astype(bf16)


def select(requests, parts):
    shape = jax.ShapeDtypeStruct((16, 1024), bf16)
    return call(
        select_kernel,
        (shape,) * 3,
        48 * 320 * 2048,
        320 * 2048 * 4,
        in_specs=[SM] * 3 + [VM] * 4,
        out_specs=[VM] * 3,
    )(*requests, *parts)


def terms_kernel(count, target, v0, v1, v2, integral, out, acc, vt):
    q = pl.program_id(0)

    @pl.when(q == 0)
    def _():
        v = v0[...].astype(f32) + v1[...].astype(f32) + v2[...].astype(f32)
        vt[:, 0:16] = v.T
        vt[:, 16:128] = jnp.zeros((1024, 112), f32)
        acc[...] = jnp.zeros_like(acc)

    lane = lax.broadcasted_iota(jnp.int32, (1024, 128), 1)
    live = q < count[0]
    side = jnp.where(jnp.logical_and(lane == q, live), vt[...], 0.0).astype(bf16)
    acc[...] += jnp.dot(integral[0], side, preferred_element_type=f32)

    @pl.when(q == QCAP - 1)
    def _():
        out[:, 0:1024] = acc[...].T[0:QCAP, :].astype(bf16)
        col = lax.broadcasted_iota(jnp.int32, (QCAP, 128), 1)
        row = lax.broadcasted_iota(jnp.int32, (QCAP, 128), 0)
        mark = jnp.zeros((QCAP, 128), jnp.int32)
        for i in range(QCAP):
            t = target[i]
            note = jnp.where(col == 0, t // KCAP, jnp.where(col == 1, t % KCAP // 32, jnp.where(col == 2, t % 32, 0)))
            mark = jnp.where(row == i, note, mark)
        out[:, 1024:EXT] = mark.astype(f32).astype(bf16)


def exchange(count, target, vectors, integrals):
    return call(
        terms_kernel,
        jax.ShapeDtypeStruct((QCAP, EXT), bf16),
        QCAP * 2 * 1024 * 1024 * 128,
        QCAP * 2 * MB,
        grid=(QCAP,),
        in_specs=[SM, SM, VM, VM, VM, pl.BlockSpec((1, 1024, 1024), lambda q: (q, 0, 0))],
        out_specs=pl.BlockSpec((QCAP, EXT), lambda q: (0, 0)),
        scratch_shapes=[pltpu.VMEM((1024, 128), f32), pltpu.VMEM((1024, 128), f32)],
    )(count, target, *vectors, integrals)


def tiles_kernel(where, f0, f1, f2, f3, t0, t1, t2, t3, t4, out, fcur, tcur, wide, spread):
    g = pl.program_id(0)
    at = here()
    for i, f in enumerate((f0, f1, f2, f3)):

        @pl.when(g == i)
        def _():
            fcur[...] = f[...]

    @pl.when(g == 0)
    def _():
        for i, t in enumerate((t0, t1, t2, t3)):
            tcur[16 * i : 16 * i + 16, :] = t[...]

    @pl.when(g == 2)
    def _():
        tcur[...] = t4[...]

    k = at["z"] * 2 + jnp.where(g % 2 == 0, at["yh"], 1 - at["yh"])
    marks = tcur[:, 1024:EXT].astype(f32)
    slot = (marks[:, 1:2] * 32.0 + marks[:, 2:3]).astype(jnp.int32)
    slot = jnp.where(marks[:, 0:1].astype(jnp.int32) == k, slot, -1)
    spots = lax.broadcasted_iota(jnp.int32, (64, KCAP), 1)
    hot = (slot == spots).astype(f32).astype(bf16)
    update = lax.dot_general(hot, tcur[:, 0:1024], (((0,), (0,)), ((), ())), preferred_element_type=f32)
    fock = (fcur[:, 0:1024].astype(f32) + 0.25 * update).astype(bf16)
    place = fcur[:, 1024:EXT].astype(f32)
    tr = place[:, 0:1].astype(jnp.int32)
    tc = place[:, 1:2].astype(jnp.int32)
    lane = lax.broadcasted_iota(jnp.int32, (KCAP, 512), 1)
    keep = (lane % 128 // BS) == (tc % 4)
    src = lax.broadcasted_iota(jnp.int32, (128, 512), 0)
    dst = lax.broadcasted_iota(jnp.int32, (128, 512), 1)
    copy = (src == dst // 128 * BS + dst % BS).astype(f32).astype(bf16)
    for a in range(8):
        piece = jnp.dot(fock[:, a * 128 : (a + 1) * 128], copy, preferred_element_type=f32)
        wide[:, a * 512 : (a + 1) * 512] = jnp.where(keep, piece, 0.0).astype(bf16)
    spot = lax.broadcasted_iota(jnp.int32, (KCAP, GROUPS * TROWS), 1)
    put = (spot == tc // 4 * TROWS + tr).astype(f32).astype(bf16)
    for h in range(8):
        spread[...] = lax.dot_general(
            put, wide[:, h * 512 : (h + 1) * 512], (((0,), (0,)), ((), ())), preferred_element_type=f32
        )
        for p in range(2):
            for t in range(GROUPS):
                pair = [
                    spread[t * TROWS : (t + 1) * TROWS, (2 * p + o) * 128 : (2 * p + o + 1) * 128]
                    for o in range(2)
                ]
                start = (4 * h + 2 * p) * TROWS
                out[start : start + 2 * TROWS, t * 128 : (t + 1) * 128] = jnp.concatenate(pair, axis=0).astype(bf16)


def tiles(focks, terms, places):
    spec = pltpu.PrefetchScalarGridSpec(
        num_scalar_prefetch=1,
        grid=(4,),
        in_specs=[VM] * 9,
        out_specs=pl.BlockSpec((ROWS, COLS), lambda g, w: (w[2 * g], w[2 * g + 1])),
        scratch_shapes=[
            pltpu.VMEM((KCAP, EXT), bf16),
            pltpu.VMEM((64, EXT), bf16),
            pltpu.VMEM((KCAP, 4096), bf16),
            pltpu.VMEM((GROUPS * TROWS, 512), f32),
        ],
    )
    return call(
        tiles_kernel,
        jax.ShapeDtypeStruct((2 * ROWS, 2 * COLS), bf16),
        10 * 10**9,
        16 * MB,
        grid_spec=spec,
    )(places, *focks, *terms)


def product_kernel(mat, own, left, right, far_a, far_b, p2t, p2b, pp, pm, p0, cols, sems):
    i = pl.program_id(0)
    at = here()

    @pl.when(i == 0)
    def _():
        copies = []
        plan = ((own, 0, 0, 2), (left, 3, 0, 2), (right, 1, 0, 2), (far_a, 2, 0, 1), (far_b, 2, 1, 1))
        for n, (ref, step, first, halves) in enumerate(plan):
            lane = pl.multiple_of((at["x"] + step - at["z"] + 4) % 4 * W, W)
            dst = cols.at[first * COLS : (first + halves) * COLS, pl.ds(lane, W)]
            copy = pltpu.make_async_copy(ref, dst, sems.at[n])
            copy.start()
            copies.append(copy)
        for copy in copies:
            copy.wait()

    full = jnp.dot(mat[...], cols[...], preferred_element_type=f32)
    p0[...] = full[:, 0:W].astype(bf16)
    pp[...] = full[:, W : 2 * W].astype(bf16)
    pm[...] = full[:, 3 * W : 4 * W].astype(bf16)

    @pl.when(i == 0)
    def _():
        p2t[...] = full[:, 2 * W : 3 * W].astype(bf16)

    @pl.when(i == 1)
    def _():
        p2b[...] = full[:, 2 * W : 3 * W].astype(bf16)


def product(mat, blocks):
    half = jax.ShapeDtypeStruct((ROWS, W), bf16)
    both = jax.ShapeDtypeStruct((2 * ROWS, W), bf16)
    fixed = pl.BlockSpec((ROWS, W), lambda i: (0, 0))
    moving = pl.BlockSpec((ROWS, W), lambda i: (i, 0))
    return call(
        product_kernel,
        (half, half, both, both, both),
        2 * 1536 * 3072 * 512,
        14 * MB,
        grid=(2,),
        in_specs=[pl.BlockSpec((ROWS, 2 * COLS), lambda i: (i, 0))] + [ANY] * 5,
        out_specs=[fixed, fixed, moving, moving, moving],
        scratch_shapes=[pltpu.VMEM((2 * COLS, 4 * W), bf16), pltpu.SemaphoreType.DMA((5,))],
    )(mat, *blocks)


def finish_kernel(k0, k1, k2, g0, g1, g2, out, joined):
    c = lax.axis_index("row") % 2
    mine = pl.multiple_of(c * (3 * W), W)
    other = pl.multiple_of((1 - c) * (3 * W), W)
    for j, (a, b) in enumerate(((k0, g0), (k1, g1), (k2, g2))):
        joined[:, pl.ds(mine + j * W, W)] = a[...]
        joined[:, pl.ds(other + j * W, W)] = b[...]
    row = lax.broadcasted_iota(jnp.int32, (ROWS, ROWS), 0)
    col = lax.broadcasted_iota(jnp.int32, (ROWS, ROWS), 1)
    order = (col == row % BS * TROWS + row // BS).astype(f32).astype(bf16)
    out[...] = jnp.dot(order, joined[...], preferred_element_type=f32).astype(bf16)


def finish(kept, got):
    return call(
        finish_kernel,
        jax.ShapeDtypeStruct((ROWS, 6 * W), bf16),
        2 * ROWS**3,
        4 * MB,
        in_specs=[VM] * 6,
        out_specs=VM,
        scratch_shapes=[pltpu.VMEM((ROWS, 6 * W), bf16)],
    )(*kept, *got)


def body(
    orbitals,
    fock_blocks,
    fock_where,
    density_blocks,
    integrals,
    quartet_density,
    quartet_target,
    quartet_count,
):
    at = here()
    with jax.named_scope("density"):
        ask_above = shift_row(quartet_density, -1)
        ask_below = shift_row(quartet_density, 1)
        pair = jnp.concatenate([density_blocks, swap_yh(density_blocks)], axis=0)
        pool = (pair, shift_z(pair, 1), shift_z(pair, -1), shift_z(pair, 2))
        own, for_above, for_below = select((quartet_density, ask_above, ask_below), pool)
        vectors = (own, shift_row(for_above, 1), shift_row(for_below, -1))
    with jax.named_scope("terms"):
        term = exchange(quartet_count, quartet_target, vectors, integrals)
        term2 = jnp.concatenate([term, swap_yh(term)], axis=0)
        row_terms = (term2, shift_z(term2, 1), shift_z(term2, -1), shift_z(term2, 2))
        other_terms = swap_core(jnp.concatenate(row_terms, axis=0))
    with jax.named_scope("fock"):
        spot = jnp.stack([fock_where // TCOLS, fock_where % TCOLS], axis=1).astype(bf16)
        fock = jnp.concatenate([fock_blocks, jnp.pad(spot, ((0, 0), (0, 126)))], axis=1)
        fock_h = swap_yh(fock)
        fock_c = swap_core(fock)
        fock_hc = swap_core(fock_h)
        own_slot = jnp.where(at["yh"] == at["yl"], 1, 0)
        c = at["c"]
        places = jnp.stack([c, own_slot, c, 1 - own_slot, 1 - c, own_slot, 1 - c, 1 - own_slot]).astype(jnp.int32)
        mat = tiles((fock, fock_h, fock_c, fock_hc), (*row_terms, other_terms), places)
    blocks = []
    for j in range(3):
        with jax.named_scope("gather"):
            piece = orbitals[:, j * W : (j + 1) * W]
            slots = jnp.concatenate([move_y(piece, (1, 3, 0, 2)), move_y(piece, (0, 2, 1, 3))], axis=0)
            left, right = shift_x(slots, 1), shift_x(slots, -1)
            far_a = shift_x(left[:COLS], 1)
            far_b = shift_x(right[COLS:], -1)
            blocks.append((slots, left, right, far_a, far_b))
    kept, got = [], []
    for j in range(3):
        with jax.named_scope("reduce"):
            p2t, p2b, pp, pm, p0 = product(mat, blocks[j])
            from_below = shift_z(p2t, 1)
            from_above = shift_z(p2b, -1)
            pp = jnp.concatenate([(pp[:ROWS].astype(f32) + from_below.astype(f32)).astype(bf16), pp[ROWS:]], axis=0)
            pm = jnp.concatenate([pm[:ROWS], (pm[ROWS:].astype(f32) + from_above.astype(f32)).astype(bf16)], axis=0)
            a, b = shift_z(pp, 1), shift_z(pm, -1)
            total = (p0.astype(f32) + a.astype(f32) + b.astype(f32)).astype(bf16).reshape(2, ROWS, W)
            kept.append(lax.dynamic_index_in_dim(total, c, 0, keepdims=False))
            got.append(swap_core(lax.dynamic_index_in_dim(total, 1 - c, 0, keepdims=False)))
    with jax.named_scope("finish"):
        return finish(kept, got)


def solution(mesh):
    return jax.shard_map(
        body,
        mesh=mesh,
        in_specs=(
            P("col", "row"),
            P(("row", "col"), None),
            P(("row", "col")),
            P(("row", "col"), None),
            P(("row", "col"), None, None),
            P(("row", "col")),
            P(("row", "col")),
            P(("row", "col")),
        ),
        out_specs=P("row", "col"),
        check_vma=False,
    )
```

```python
import functools

import jax
import jax.numpy as jnp
from jax import lax
from jax.experimental import pallas as pl
from jax.experimental.pallas import tpu as pltpu
from jax.sharding import PartitionSpec as P

BS = 32
TROWS, TCOLS = 24, 48
KCAP, PCAP, QCAP = 512, 40, 8
ROWS, COLS = TROWS * BS, TCOLS * BS
GROUPS = TCOLS // 4
EXT = 1024 + 128
W = 128
AXES = ("row", "col")
SLOT_A, SLOT_B = (1, 3, 0, 2), (0, 2, 1, 3)
MB = 1 << 20
bf16, f32 = jnp.bfloat16, jnp.float32


def coords(d):
    r, k = d // 8, d % 8
    return dict(x=r // 4, yl=r // 2 % 2, c=r % 2, z=k // 2, yh=k % 2)


def number(x, yl, c, z, yh):
    return ((x % 4) * 4 + yl * 2 + c) * 8 + (z % 4) * 2 + yh


def move(value, to):
    pairs = []
    for d in range(128):
        place = coords(d)
        target = dict(place)
        target.update(to(**place))
        pairs.append((d, number(**target)))
    return lax.ppermute(value, AXES, pairs)


def shift_x(value, by):
    return move(value, lambda x, **o: dict(x=x + by))


def shift_z(value, by):
    return move(value, lambda z, **o: dict(z=z + by))


def swap_z(value, by):
    return move(value, lambda z, **o: dict(z=z ^ by))


def swap_core(value):
    return move(value, lambda c, **o: dict(c=1 - c))


def swap_yh(value):
    return move(value, lambda yh, **o: dict(yh=1 - yh))


def shift_row(value, by):
    pairs = [(d, (d + 8 * by) % 128) for d in range(128)]
    return lax.ppermute(value, AXES, pairs)


def move_y(value, table):
    def to(yl, yh, **o):
        y = table[yh * 2 + yl]
        return dict(yl=y % 2, yh=y // 2)

    return move(value, to)


def here():
    r, k = lax.axis_index("row"), lax.axis_index("col")
    return dict(r=r, k=k, x=r // 4, yl=r // 2 % 2, c=r % 2, z=k // 2, yh=k % 2)


def call(kernel, out_shape, vmem, *, in_specs, after=(), gflop=0, **kw):
    n = len(after)
    run = pl.pallas_call(
        lambda *refs: kernel(*refs[n:]),
        out_shape=out_shape,
        in_specs=[ANY] * n + list(in_specs),
        compiler_params=pltpu.CompilerParams(vmem_limit_bytes=vmem * MB),
        cost_estimate=pl.CostEstimate(flops=gflop * 10**9 + 1, bytes_accessed=1, transcendentals=0),
        **kw,
    )
    return lambda *operands: run(*after, *operands)


VM = pl.BlockSpec(memory_space=pltpu.VMEM)
SM = pl.BlockSpec(memory_space=pltpu.SMEM)
ANY = pl.BlockSpec(memory_space=pl.ANY)


def select_kernel(req_own, req_a, req_b, p0, p1, p2, p3, out_own, out_a, out_b):
    at = here()
    parts = (p0, p1, p2, p3)
    steps = (0, 3, 1, 2)
    span = 2 * PCAP
    lane = lax.broadcasted_iota(jnp.int32, (16, span), 1)
    row = lax.broadcasted_iota(jnp.int32, (16, span), 0)
    for req, out in ((req_own, out_own), (req_a, out_a), (req_b, out_b)):
        want = jnp.full((16, span), -1, jnp.int32)
        for q in range(QCAP):
            want = jnp.where(row == q, req[q], want)
        total = jnp.zeros((16, 1024), f32)
        for part, step in zip(parts, steps):
            z = (at["z"] + step) % 4
            yh = jnp.where(lane < PCAP, at["yh"], 1 - at["yh"])
            held = (at["r"] * 8 + z * 2 + yh) * PCAP + jnp.where(lane < PCAP, lane, lane - PCAP)
            hot = (want == held).astype(f32).astype(bf16)
            total = total + jnp.dot(hot, part[...], preferred_element_type=f32)
        out[...] = total.astype(bf16)


def select(requests, parts):
    shape = jax.ShapeDtypeStruct((16, 1024), bf16)
    return call(
        select_kernel,
        (shape,) * 3,
        6,
        in_specs=[SM] * 3 + [VM] * 4,
        out_specs=[VM] * 3,
    )(*requests, *parts)


def terms_kernel(count, target, v0, v1, v2, integral, out, buf, sems):
    def fetch(q):
        return pltpu.make_async_copy(integral.at[q], buf.at[q], sems.at[q])

    for q in range(QCAP):
        fetch(q).start()
    out[...] = jnp.zeros_like(out)
    col = lax.broadcasted_iota(jnp.int32, (QCAP, 128), 1)
    row = lax.broadcasted_iota(jnp.int32, (QCAP, 128), 0)
    mark = jnp.zeros((QCAP, 128), jnp.int32)
    core = here()["c"]
    for i in range(QCAP):
        t = target[i]
        note = jnp.where(col == 0, t // KCAP, jnp.where(col == 1, t % KCAP // 32, jnp.where(col == 2, t % 32, core)))
        mark = jnp.where(row == i, note, mark)
    out[:, 1024:EXT] = mark.astype(f32).astype(bf16)
    v = v0[...].astype(f32) + v1[...].astype(f32) + v2[...].astype(f32)
    rows = lax.broadcasted_iota(jnp.int32, (16, 1024), 0)
    places = lax.broadcasted_iota(jnp.int32, (QCAP, 1024), 0)

    def one(q, carry):
        fetch(q).wait()
        vector = jnp.sum(jnp.where(rows == q, v, 0.0), axis=0, keepdims=True)
        sums = []
        for h in range(2):
            acc = jnp.zeros((512, 128), f32)
            for a in range(8):
                lanes = slice(a * 128, (a + 1) * 128)
                acc = acc + buf[q, h * 512 : (h + 1) * 512, lanes].astype(f32) * vector[:, lanes]
            sums.append(jnp.sum(acc.T, axis=0, keepdims=True))
        term = jnp.where(q < count[0], jnp.concatenate(sums, axis=1), 0.0)
        out[:, 0:1024] = jnp.where(places == q, term, out[:, 0:1024].astype(f32)).astype(bf16)
        return carry

    lax.fori_loop(0, QCAP, one, 0)


def exchange(count, target, vectors, integrals):
    return call(
        terms_kernel,
        jax.ShapeDtypeStruct((QCAP, EXT), bf16),
        48,
        in_specs=[SM, SM, VM, VM, VM, ANY],
        out_specs=VM,
        scratch_shapes=[pltpu.VMEM((QCAP, 1024, 1024), bf16), pltpu.SemaphoreType.DMA((QCAP,))],
    )(count, target, *vectors, integrals)


def tiles_kernel(near, f0, f1, t0, t1, out, f, tcur, wide, spread):
    g = pl.program_id(0)
    at = here()
    for i, stored in enumerate((f0, f1)):

        @pl.when(g == i)
        def _():
            f[...] = stored[...]

    @pl.when(g == 0)
    def _():
        for i, t in enumerate((t0, t1)):
            tcur[64 * i : 64 * i + 64, :] = t[...]

    k = at["z"] * 2 + (at["yh"] if near else 1 - at["yh"])
    marks = tcur[:, 1024:EXT].astype(f32)
    slot = (marks[:, 1:2] * 32.0 + marks[:, 2:3]).astype(jnp.int32)
    core = jnp.where(g == 0, at["c"], 1 - at["c"])
    slot = jnp.where(marks[:, 0:1].astype(jnp.int32) == k, slot, -1)
    slot = jnp.where(marks[:, 3:4].astype(jnp.int32) == core, slot, -1)
    spots = lax.broadcasted_iota(jnp.int32, (128, KCAP), 1)
    hot = (slot == spots).astype(f32).astype(bf16)
    update = lax.dot_general(hot, tcur[:, 0:1024], (((0,), (0,)), ((), ())), preferred_element_type=f32)
    fock = (f[:, 0:1024].astype(f32) + 0.25 * update).astype(bf16)
    place = f[:, 1024:EXT].astype(f32)
    tr = place[:, 0:1].astype(jnp.int32)
    tc = place[:, 1:2].astype(jnp.int32)
    lane = lax.broadcasted_iota(jnp.int32, (KCAP, 512), 1)
    keep = (lane % 128 // BS) == (tc % 4)
    src = lax.broadcasted_iota(jnp.int32, (128, 512), 0)
    dst = lax.broadcasted_iota(jnp.int32, (128, 512), 1)
    copy = (src == dst // 128 * BS + dst % BS).astype(f32).astype(bf16)
    for a in range(8):
        piece = jnp.dot(fock[:, a * 128 : (a + 1) * 128], copy, preferred_element_type=f32)
        wide[:, a * 512 : (a + 1) * 512] = jnp.where(keep, piece, 0.0).astype(bf16)
    spot = lax.broadcasted_iota(jnp.int32, (KCAP, GROUPS * TROWS), 1)
    put = (spot == tc // 4 * TROWS + tr).astype(f32).astype(bf16)
    for h in range(8):
        spread[...] = lax.dot_general(
            put, wide[:, h * 512 : (h + 1) * 512], (((0,), (0,)), ((), ())), preferred_element_type=f32
        )
        for p in range(2):
            for t in range(GROUPS):
                pair = [
                    spread[t * TROWS : (t + 1) * TROWS, (2 * p + o) * 128 : (2 * p + o + 1) * 128]
                    for o in range(2)
                ]
                start = (4 * h + 2 * p) * TROWS
                out[start : start + 2 * TROWS, t * 128 : (t + 1) * 128] = jnp.concatenate(pair, axis=0).astype(bf16)


def tiles(near, focks, terms, after, gflop=0):
    return call(
        functools.partial(tiles_kernel, near),
        jax.ShapeDtypeStruct((2 * ROWS, COLS), bf16),
        24,
        after=after,
        gflop=gflop,
        grid=(2,),
        in_specs=[VM] * 4,
        out_specs=pl.BlockSpec((ROWS, COLS), lambda g: (g, 0)),
        scratch_shapes=[
            pltpu.VMEM((KCAP, EXT), bf16),
            pltpu.VMEM((128, EXT), bf16),
            pltpu.VMEM((KCAP, 4096), bf16),
            pltpu.VMEM((GROUPS * TROWS, 512), f32),
        ],
    )(*focks, *terms)


def pack_kernel(blocks, where, out):
    out[:, 0:1024] = blocks[...]
    columns = jnp.concatenate([where[...], where[...]], axis=0).astype(f32).T.astype(jnp.int32)
    spot = jnp.concatenate([columns[:, j : j + 1] for j in range(KCAP // 128)], axis=0)
    lane = lax.broadcasted_iota(jnp.int32, (KCAP, 128), 1)
    note = jnp.where(lane == 0, spot // TCOLS, jnp.where(lane == 1, spot % TCOLS, 0))
    out[:, 1024:EXT] = note.astype(f32).astype(bf16)


def pack(blocks, where):
    return call(
        pack_kernel,
        jax.ShapeDtypeStruct((KCAP, EXT), bf16),
        8,
        in_specs=[VM] * 2,
        out_specs=VM,
    )(blocks, where.reshape(KCAP // 128, 128))


def hold_kernel(value, out, sem):
    copy = pltpu.make_async_copy(value, out, sem)
    copy.start()
    copy.wait()


def hold(value, after):
    return call(
        hold_kernel,
        jax.ShapeDtypeStruct(value.shape, value.dtype),
        2,
        after=after,
        in_specs=[ANY],
        out_specs=ANY,
        scratch_shapes=[pltpu.SemaphoreType.DMA],
    )(value)


def cut_kernel(j, value, out, sem):
    copy = pltpu.make_async_copy(value.at[:, j * W : (j + 1) * W], out, sem)
    copy.start()
    copy.wait()


def cut(value, j, after):
    return call(
        functools.partial(cut_kernel, j),
        jax.ShapeDtypeStruct((COLS, W), bf16),
        2,
        after=after,
        in_specs=[ANY],
        out_specs=ANY,
        scratch_shapes=[pltpu.SemaphoreType.DMA],
    )(value)


def join_kernel(a, b, out, sems):
    copies = [pltpu.make_async_copy(src, out.at[i * COLS : (i + 1) * COLS], sems.at[i]) for i, src in enumerate((a, b))]
    for copy in copies:
        copy.start()
    for copy in copies:
        copy.wait()


def join(a, b, after):
    return call(
        join_kernel,
        jax.ShapeDtypeStruct((2 * COLS, W), bf16),
        2,
        after=after,
        in_specs=[ANY] * 2,
        out_specs=ANY,
        scratch_shapes=[pltpu.SemaphoreType.DMA((2,))],
    )(a, b)


def turned(orbitals, j, before, after):
    piece = cut(orbitals, j, before)
    return join(move_y(piece, SLOT_A), move_y(piece, SLOT_B), after)


def product_kernel(sizes, steps, near, far, *refs):
    at = here()
    n = len(sizes)
    wide = n * W
    blocks, outs, cols, sems = refs[: sum(sizes)], refs[sum(sizes) : -2], refs[-2], refs[-1]
    first = jnp.where(at["yh"] == at["yl"], COLS, 0)
    copies = []
    base = 0
    for j, size in enumerate(sizes):
        plan = [(b, s, h, h * COLS) for b, s in ((0, 0), (1, 3), (2, 1)) for h in range(2)]
        if size == 4:
            plan += [(3, 2, 0, 0), (3, 2, 1, COLS)]
        else:
            plan += [(3, 2, 0, 0), (4, 2, 1, 0)]
        for b, step, slot, start in plan:
            to = (at["x"] + step - at["z"] + 4) % 4
            wanted, place = to == steps[0], 0
            for i, other in enumerate(steps[1:]):
                wanted = jnp.logical_or(wanted, to == other)
                place = jnp.where(to == other, i + 1, place)
            lane = pl.multiple_of((place * n + j) * W, W)
            row = pl.multiple_of(first if slot == 0 else COLS - first, COLS)
            dst = cols.at[pl.ds(row, COLS), pl.ds(lane, W)]
            copy = pltpu.make_async_copy(blocks[base + b].at[start : start + COLS], dst, sems.at[len(copies)])
            copies.append((wanted, copy))
        base += size
    for wanted, copy in copies:

        @pl.when(wanted)
        def _():
            copy.start()

    for wanted, copy in copies:

        @pl.when(wanted)
        def _():
            copy.wait()

    for i in range(2):
        rows = slice(i * ROWS, (i + 1) * ROWS)
        part = jnp.dot(near[rows, :], cols[:COLS, :], preferred_element_type=f32)
        part = (part + jnp.dot(far[rows, :], cols[COLS:, :], preferred_element_type=f32)).astype(bf16)
        for o, out in enumerate(outs):
            out[rows, :] = part[:, o * wide : (o + 1) * wide]


def product(mats, chunks, steps, after=(), gflop=0):
    n = len(chunks)
    sizes = tuple(len(c) for c in chunks)
    return call(
        functools.partial(product_kernel, sizes, steps),
        (jax.ShapeDtypeStruct((2 * ROWS, n * W), bf16),) * len(steps),
        24,
        after=after,
        gflop=gflop,
        in_specs=[VM] * 2 + [ANY] * sum(sizes),
        out_specs=[VM] * len(steps),
        scratch_shapes=[pltpu.VMEM((2 * COLS, len(steps) * n * W), bf16), pltpu.SemaphoreType.DMA((8 * n,))],
    )(*mats, *(b for c in chunks for b in c))


def merge_kernel(pp, pm, above, below, pp_out, pm_out):
    pp_out[:ROWS, :] = (pp[:ROWS, :].astype(f32) + above[...].astype(f32)).astype(bf16)
    pp_out[ROWS:, :] = pp[ROWS:, :]
    pm_out[:ROWS, :] = pm[:ROWS, :]
    pm_out[ROWS:, :] = (pm[ROWS:, :].astype(f32) + below[...].astype(f32)).astype(bf16)


def merge(pp, pm, above, below, after):
    shape = jax.ShapeDtypeStruct(pp.shape, bf16)
    return call(merge_kernel, (shape, shape), 8, after=after, in_specs=[VM] * 4, out_specs=[VM] * 2)(
        pp, pm, above, below
    )


def settle_kernel(p0, a, b, keep, send):
    for out, start in ((send, ROWS), (keep, 0)):
        rows = slice(start, start + ROWS)
        total = p0[rows, :].astype(f32) + a[rows, :].astype(f32) + b[rows, :].astype(f32)
        out[...] = total.astype(bf16)


def settle(p0, a, b):
    shape = jax.ShapeDtypeStruct((ROWS, p0.shape[1]), bf16)
    return call(settle_kernel, (shape, shape), 8, in_specs=[VM] * 3, out_specs=[VM] * 2)(p0, a, b)


def finish_kernel(k0, k1, g0, g1, out, joined):
    c = lax.axis_index("row") % 2
    mine = pl.multiple_of(c * (3 * W), W)
    other = pl.multiple_of((1 - c) * (3 * W), W)
    for base, first, last in ((mine, k0, k1), (other, g0, g1)):
        joined[:, pl.ds(base, 2 * W)] = first[...]
        joined[:, pl.ds(pl.multiple_of(base + 2 * W, W), W)] = last[...]
    row = lax.broadcasted_iota(jnp.int32, (ROWS, ROWS), 0)
    col = lax.broadcasted_iota(jnp.int32, (ROWS, ROWS), 1)
    order = (col == row % BS * TROWS + row // BS).astype(f32).astype(bf16)
    out[...] = jnp.dot(order, joined[...], preferred_element_type=f32).astype(bf16)


def finish(kept, got):
    return call(
        finish_kernel,
        jax.ShapeDtypeStruct((ROWS, 6 * W), bf16),
        16,
        in_specs=[VM] * 4,
        out_specs=VM,
        scratch_shapes=[pltpu.VMEM((ROWS, 6 * W), bf16)],
    )(*kept, *got)


def body(
    orbitals,
    fock_blocks,
    fock_where,
    density_blocks,
    integrals,
    quartet_density,
    quartet_target,
    quartet_count,
):
    with jax.named_scope("fock"):
        fock = pack(fock_blocks, fock_where)
    with jax.named_scope("density"):
        ask_above = shift_row(quartet_density, -1)
        ask_below = shift_row(quartet_density, 1)
        pair = jnp.concatenate([density_blocks, swap_yh(density_blocks)], axis=0)
        piece0 = cut(orbitals, 0, (pair, ask_above, ask_below))
        moved0 = (move_y(piece0, SLOT_A), move_y(piece0, SLOT_B))
        pool = (pair, shift_z(pair, 1), shift_z(pair, -1), shift_z(pair, 2))
        own, for_above, for_below = select((quartet_density, ask_above, ask_below), pool)
        vectors = (own, shift_row(for_above, 1), shift_row(for_below, -1))
    with jax.named_scope("gather"):
        slots0 = join(*moved0, vectors[1:])
        left0, right0 = shift_x(slots0, 1), shift_x(slots0, -1)
        term = exchange(quartet_count, quartet_target, vectors, integrals)
        slots1 = turned(orbitals, 1, (*vectors[1:], fock), (term,))
        left1, right1 = shift_x(slots1, 1), shift_x(slots1, -1)
        far0, far1 = shift_x(left0, 1), shift_x(right1, -1)
    with jax.named_scope("terms"):
        term = hold(term, (slots1, left0, right0))
        term = jnp.concatenate([term, swap_yh(term)], axis=0)
    with jax.named_scope("fock"):
        fock_h = swap_yh(hold(fock, (term,)))
    with jax.named_scope("terms"):
        term = hold(term, (left1, right1))
        term = jnp.concatenate([term, swap_z(term, 1)], axis=0)
        term = jnp.concatenate([term, swap_z(term, 2)], axis=0)
        terms = (term, swap_core(term))
    with jax.named_scope("fock"):
        fock_h = hold(fock_h, (term,))
        near = tiles(True, (fock, swap_core(fock)), terms, (), 20)
        far = tiles(False, (fock_h, swap_core(fock_h)), terms, (far0, far1))
        mats = (near, far)
    with jax.named_scope("gather"):
        slots2 = turned(orbitals, 2, (fock_h,), (far0, far1, near))
        left2, right2 = shift_x(slots2, 1), shift_x(slots2, -1)
    kept, got, mixed = [], [], ()
    for n in (2, 1):
        if n == 2:
            chunks = ((slots0, left0, right0, far0), (slots1, left1, right1, far1))
        else:
            with jax.named_scope("gather"):
                far2a = shift_x(hold(left2[:COLS], mixed), 1)
                far2b = shift_x(hold(right2[COLS:], mixed), -1)
            chunks = ((slots2, left2, right2, far2a, far2b),)
        with jax.named_scope("reduce"):
            (p2,) = product(mats, chunks, (2,), mixed)
            above, below = shift_z(p2[:ROWS], 1), shift_z(p2[ROWS:], -1)
            pp, pm = product(mats, chunks, (1, 3), tuple(kept), 20)
            pp, pm = merge(pp, pm, above, below, (left2, right2))
            mixed = (pp, pm)
            (p0,) = product(mats, chunks, (0,), mixed, 20)
            keep, send = settle(p0, shift_z(pp, 1), shift_z(pm, -1))
            kept.append(keep)
            got.append(swap_core(send))
    with jax.named_scope("finish"):
        return finish(kept, got)


def solution(mesh):
    return jax.shard_map(
        body,
        mesh=mesh,
        in_specs=(
            P("col", "row"),
            P(("row", "col"), None),
            P(("row", "col")),
            P(("row", "col"), None),
            P(("row", "col"), None, None),
            P(("row", "col")),
            P(("row", "col")),
            P(("row", "col")),
        ),
        out_specs=P("row", "col"),
        check_vma=False,
    )
```

```python
import functools

import jax
import jax.numpy as jnp
from jax import lax
from jax.experimental import pallas as pl
from jax.experimental.pallas import tpu as pltpu
from jax.sharding import PartitionSpec as P

BS = 32
TROWS, TCOLS = 24, 48
KCAP, PCAP, QCAP = 512, 40, 8
ROWS, COLS = TROWS * BS, TCOLS * BS
GROUPS = TCOLS // 4
EXT = 1024 + 128
W = 128
AXES = ("row", "col")
SLOT_A, SLOT_B = (1, 3, 0, 2), (0, 2, 1, 3)
MB = 1 << 20
bf16, f32 = jnp.bfloat16, jnp.float32


def coords(d):
    r, k = d // 8, d % 8
    return dict(x=r // 4, yl=r // 2 % 2, c=r % 2, z=k // 2, yh=k % 2)


def number(x, yl, c, z, yh):
    return ((x % 4) * 4 + yl * 2 + c) * 8 + (z % 4) * 2 + yh


def move(value, to):
    pairs = []
    for d in range(128):
        place = coords(d)
        target = dict(place)
        target.update(to(**place))
        pairs.append((d, number(**target)))
    return lax.ppermute(value, AXES, pairs)


def shift_x(value, by):
    return move(value, lambda x, **o: dict(x=x + by))


def shift_z(value, by):
    return move(value, lambda z, **o: dict(z=z + by))


def swap_z(value, by):
    return move(value, lambda z, **o: dict(z=z ^ by))


def swap_core(value):
    return move(value, lambda c, **o: dict(c=1 - c))


def swap_yh(value):
    return move(value, lambda yh, **o: dict(yh=1 - yh))


def shift_row(value, by):
    pairs = [(d, (d + 8 * by) % 128) for d in range(128)]
    return lax.ppermute(value, AXES, pairs)


def move_y(value, table):
    def to(yl, yh, **o):
        y = table[yh * 2 + yl]
        return dict(yl=y % 2, yh=y // 2)

    return move(value, to)


def here():
    r, k = lax.axis_index("row"), lax.axis_index("col")
    return dict(r=r, k=k, x=r // 4, yl=r // 2 % 2, c=r % 2, z=k // 2, yh=k % 2)


def call(kernel, out_shape, vmem, *, in_specs, after=(), gflop=0, **kw):
    n = len(after)
    run = pl.pallas_call(
        lambda *refs: kernel(*refs[n:]),
        out_shape=out_shape,
        in_specs=[ANY] * n + list(in_specs),
        compiler_params=pltpu.CompilerParams(vmem_limit_bytes=vmem * MB),
        cost_estimate=pl.CostEstimate(flops=gflop * 10**9 + 1, bytes_accessed=1, transcendentals=0),
        **kw,
    )
    return lambda *operands: run(*after, *operands)


VM = pl.BlockSpec(memory_space=pltpu.VMEM)
SM = pl.BlockSpec(memory_space=pltpu.SMEM)
ANY = pl.BlockSpec(memory_space=pl.ANY)


def select_kernel(req_own, req_a, req_b, p0, p1, p2, p3, out_own, out_a, out_b):
    at = here()
    parts = (p0, p1, p2, p3)
    steps = (0, 3, 1, 2)
    span = 2 * PCAP
    lane = lax.broadcasted_iota(jnp.int32, (16, span), 1)
    row = lax.broadcasted_iota(jnp.int32, (16, span), 0)
    for req, out in ((req_own, out_own), (req_a, out_a), (req_b, out_b)):
        want = jnp.full((16, span), -1, jnp.int32)
        for q in range(QCAP):
            want = jnp.where(row == q, req[q], want)
        total = jnp.zeros((16, 1024), f32)
        for part, step in zip(parts, steps):
            z = (at["z"] + step) % 4
            yh = jnp.where(lane < PCAP, at["yh"], 1 - at["yh"])
            held = (at["r"] * 8 + z * 2 + yh) * PCAP + jnp.where(lane < PCAP, lane, lane - PCAP)
            hot = (want == held).astype(f32).astype(bf16)
            total = total + jnp.dot(hot, part[...], preferred_element_type=f32)
        out[...] = total.astype(bf16)


def select(requests, parts):
    shape = jax.ShapeDtypeStruct((16, 1024), bf16)
    return call(
        select_kernel,
        (shape,) * 3,
        6,
        in_specs=[SM] * 3 + [VM] * 4,
        out_specs=[VM] * 3,
    )(*requests, *parts)


def terms_kernel(count, target, v0, v1, v2, integral, out, buf, sems):
    def fetch(q):
        return pltpu.make_async_copy(integral.at[q], buf.at[q], sems.at[q])

    for q in range(QCAP):
        fetch(q).start()
    out[...] = jnp.zeros_like(out)
    col = lax.broadcasted_iota(jnp.int32, (QCAP, 128), 1)
    row = lax.broadcasted_iota(jnp.int32, (QCAP, 128), 0)
    mark = jnp.zeros((QCAP, 128), jnp.int32)
    core = here()["c"]
    for i in range(QCAP):
        t = target[i]
        note = jnp.where(col == 0, t // KCAP, jnp.where(col == 1, t % KCAP // 32, jnp.where(col == 2, t % 32, core)))
        mark = jnp.where(row == i, note, mark)
    out[:, 1024:EXT] = mark.astype(f32).astype(bf16)
    v = v0[...].astype(f32) + v1[...].astype(f32) + v2[...].astype(f32)
    rows = lax.broadcasted_iota(jnp.int32, (16, 1024), 0)
    places = lax.broadcasted_iota(jnp.int32, (QCAP, 1024), 0)

    def one(q, carry):
        fetch(q).wait()
        vector = jnp.sum(jnp.where(rows == q, v, 0.0), axis=0, keepdims=True)
        sums = []
        for h in range(2):
            acc = jnp.zeros((512, 128), f32)
            for a in range(8):
                lanes = slice(a * 128, (a + 1) * 128)
                acc = acc + buf[q, h * 512 : (h + 1) * 512, lanes].astype(f32) * vector[:, lanes]
            sums.append(jnp.sum(acc.T, axis=0, keepdims=True))
        term = jnp.where(q < count[0], jnp.concatenate(sums, axis=1), 0.0)
        out[:, 0:1024] = jnp.where(places == q, term, out[:, 0:1024].astype(f32)).astype(bf16)
        return carry

    lax.fori_loop(0, QCAP, one, 0)


def exchange(count, target, vectors, integrals):
    return call(
        terms_kernel,
        jax.ShapeDtypeStruct((QCAP, EXT), bf16),
        48,
        in_specs=[SM, SM, VM, VM, VM, ANY],
        out_specs=VM,
        scratch_shapes=[pltpu.VMEM((QCAP, 1024, 1024), bf16), pltpu.SemaphoreType.DMA((QCAP,))],
    )(count, target, *vectors, integrals)


def tiles_kernel(near, f0, f1, t0, t1, out, f, tcur, wide, spread):
    g = pl.program_id(0)
    at = here()
    for i, stored in enumerate((f0, f1)):

        @pl.when(g == i)
        def _():
            f[...] = stored[...]

    @pl.when(g == 0)
    def _():
        for i, t in enumerate((t0, t1)):
            tcur[64 * i : 64 * i + 64, :] = t[...]

    k = at["z"] * 2 + (at["yh"] if near else 1 - at["yh"])
    marks = tcur[:, 1024:EXT].astype(f32)
    slot = (marks[:, 1:2] * 32.0 + marks[:, 2:3]).astype(jnp.int32)
    core = jnp.where(g == 0, at["c"], 1 - at["c"])
    slot = jnp.where(marks[:, 0:1].astype(jnp.int32) == k, slot, -1)
    slot = jnp.where(marks[:, 3:4].astype(jnp.int32) == core, slot, -1)
    spots = lax.broadcasted_iota(jnp.int32, (128, KCAP), 1)
    hot = (slot == spots).astype(f32).astype(bf16)
    update = lax.dot_general(hot, tcur[:, 0:1024], (((0,), (0,)), ((), ())), preferred_element_type=f32)
    fock = (f[:KCAP, :].astype(f32) + 0.25 * update).astype(bf16)
    place = f[KCAP:, :KCAP].astype(f32).T
    tr = place[:, 0:1].astype(jnp.int32)
    tc = place[:, 1:2].astype(jnp.int32)
    lane = lax.broadcasted_iota(jnp.int32, (KCAP, 512), 1)
    keep = (lane % 128 // BS) == (tc % 4)
    src = lax.broadcasted_iota(jnp.int32, (128, 512), 0)
    dst = lax.broadcasted_iota(jnp.int32, (128, 512), 1)
    copy = (src == dst // 128 * BS + dst % BS).astype(f32).astype(bf16)
    for a in range(8):
        piece = jnp.dot(fock[:, a * 128 : (a + 1) * 128], copy, preferred_element_type=f32)
        wide[:, a * 512 : (a + 1) * 512] = jnp.where(keep, piece, 0.0).astype(bf16)
    spot = lax.broadcasted_iota(jnp.int32, (KCAP, GROUPS * TROWS), 1)
    put = (spot == tc // 4 * TROWS + tr).astype(f32).astype(bf16)
    for h in range(8):
        spread[...] = lax.dot_general(
            put, wide[:, h * 512 : (h + 1) * 512], (((0,), (0,)), ((), ())), preferred_element_type=f32
        )
        for p in range(2):
            for t in range(GROUPS):
                pair = [
                    spread[t * TROWS : (t + 1) * TROWS, (2 * p + o) * 128 : (2 * p + o + 1) * 128]
                    for o in range(2)
                ]
                start = (4 * h + 2 * p) * TROWS
                out[start : start + 2 * TROWS, t * 128 : (t + 1) * 128] = jnp.concatenate(pair, axis=0).astype(bf16)


def tiles(near, focks, terms, after, gflop=0):
    return call(
        functools.partial(tiles_kernel, near),
        jax.ShapeDtypeStruct((2 * ROWS, COLS), bf16),
        24,
        after=after,
        gflop=gflop,
        grid=(2,),
        in_specs=[VM] * 4,
        out_specs=pl.BlockSpec((ROWS, COLS), lambda g: (g, 0)),
        scratch_shapes=[
            pltpu.VMEM((KCAP + 16, 1024), bf16),
            pltpu.VMEM((128, EXT), bf16),
            pltpu.VMEM((KCAP, 4096), bf16),
            pltpu.VMEM((GROUPS * TROWS, 512), f32),
        ],
    )(*focks, *terms)


def pack_kernel(blocks, where, out):
    out[:KCAP, :] = blocks[...]
    spot = jnp.concatenate([where[j : j + 1, :] for j in range(KCAP // 128)], axis=1)
    row = lax.broadcasted_iota(jnp.int32, (16, KCAP), 0)
    note = jnp.where(row == 0, spot // TCOLS, jnp.where(row == 1, spot % TCOLS, 0))
    out[KCAP:, :KCAP] = note.astype(f32).astype(bf16)
    out[KCAP:, KCAP:] = jnp.zeros((16, 1024 - KCAP), bf16)


def pack(blocks, where):
    return call(
        pack_kernel,
        jax.ShapeDtypeStruct((KCAP + 16, 1024), bf16),
        8,
        in_specs=[VM] * 2,
        out_specs=VM,
    )(blocks, where.reshape(KCAP // 128, 128))


def hold_kernel(start, value, out, sem):
    copy = pltpu.make_async_copy(value.at[start : start + out.shape[0]], out, sem)
    copy.start()
    copy.wait()


def hold(value, after, start=0, rows=None):
    return call(
        functools.partial(hold_kernel, start),
        jax.ShapeDtypeStruct((rows or value.shape[0], *value.shape[1:]), value.dtype),
        2,
        after=after,
        in_specs=[ANY],
        out_specs=ANY,
        scratch_shapes=[pltpu.SemaphoreType.DMA],
    )(value)


def cut_kernel(j, value, out, sem):
    copy = pltpu.make_async_copy(value.at[:, j * W : (j + 1) * W], out, sem)
    copy.start()
    copy.wait()


def cut(value, j, after):
    return call(
        functools.partial(cut_kernel, j),
        jax.ShapeDtypeStruct((COLS, W), bf16),
        2,
        after=after,
        in_specs=[ANY],
        out_specs=ANY,
        scratch_shapes=[pltpu.SemaphoreType.DMA],
    )(value)


def join_kernel(a, b, out, sems):
    copies = [pltpu.make_async_copy(src, out.at[i * COLS : (i + 1) * COLS], sems.at[i]) for i, src in enumerate((a, b))]
    for copy in copies:
        copy.start()
    for copy in copies:
        copy.wait()


def join(a, b, after):
    return call(
        join_kernel,
        jax.ShapeDtypeStruct((2 * COLS, W), bf16),
        2,
        after=after,
        in_specs=[ANY] * 2,
        out_specs=ANY,
        scratch_shapes=[pltpu.SemaphoreType.DMA((2,))],
    )(a, b)


def turned(orbitals, j, after):
    piece = cut(orbitals, j, after)
    return move_y(piece, SLOT_A), move_y(piece, SLOT_B)


def product_kernel(sizes, steps, near, far, *refs):
    at = here()
    n = len(sizes)
    wide = n * W
    blocks, outs, cols, sems = refs[: sum(sizes)], refs[sum(sizes) : -2], refs[-2], refs[-1]
    first = jnp.where(at["yh"] == at["yl"], COLS, 0)
    copies = []
    base = 0
    for j, size in enumerate(sizes):
        plan = [(b, s, h, h * COLS) for b, s in ((0, 0), (1, 3), (2, 1)) for h in range(2)]
        if size == 4:
            plan += [(3, 2, 0, 0), (3, 2, 1, COLS)]
        else:
            plan += [(3, 2, 0, 0), (4, 2, 1, 0)]
        for b, step, slot, start in plan:
            to = (at["x"] + step - at["z"] + 4) % 4
            wanted, place = to == steps[0], 0
            for i, other in enumerate(steps[1:]):
                wanted = jnp.logical_or(wanted, to == other)
                place = jnp.where(to == other, i + 1, place)
            lane = pl.multiple_of((place * n + j) * W, W)
            row = pl.multiple_of(first if slot == 0 else COLS - first, COLS)
            dst = cols.at[pl.ds(row, COLS), pl.ds(lane, W)]
            copy = pltpu.make_async_copy(blocks[base + b].at[start : start + COLS], dst, sems.at[len(copies)])
            copies.append((wanted, copy))
        base += size
    for wanted, copy in copies:

        @pl.when(wanted)
        def _():
            copy.start()

    for wanted, copy in copies:

        @pl.when(wanted)
        def _():
            copy.wait()

    for i in range(2):
        rows = slice(i * ROWS, (i + 1) * ROWS)
        part = jnp.dot(near[rows, :], cols[:COLS, :], preferred_element_type=f32)
        part = (part + jnp.dot(far[rows, :], cols[COLS:, :], preferred_element_type=f32)).astype(bf16)
        for o, out in enumerate(outs):
            out[rows, :] = part[:, o * wide : (o + 1) * wide]


def product(mats, chunks, steps, after=(), gflop=0):
    n = len(chunks)
    sizes = tuple(len(c) for c in chunks)
    return call(
        functools.partial(product_kernel, sizes, steps),
        (jax.ShapeDtypeStruct((2 * ROWS, n * W), bf16),) * len(steps),
        24,
        after=after,
        gflop=gflop,
        in_specs=[VM] * 2 + [ANY] * sum(sizes),
        out_specs=[VM] * len(steps),
        scratch_shapes=[pltpu.VMEM((2 * COLS, len(steps) * n * W), bf16), pltpu.SemaphoreType.DMA((8 * n,))],
    )(*mats, *(b for c in chunks for b in c))


def merge_kernel(pp, pm, above, below, pp_out, pm_out):
    pp_out[:ROWS, :] = (pp[:ROWS, :].astype(f32) + above[...].astype(f32)).astype(bf16)
    pp_out[ROWS:, :] = pp[ROWS:, :]
    pm_out[:ROWS, :] = pm[:ROWS, :]
    pm_out[ROWS:, :] = (pm[ROWS:, :].astype(f32) + below[...].astype(f32)).astype(bf16)


def merge(pp, pm, above, below, after):
    shape = jax.ShapeDtypeStruct(pp.shape, bf16)
    return call(merge_kernel, (shape, shape), 8, after=after, in_specs=[VM] * 4, out_specs=[VM] * 2)(
        pp, pm, above, below
    )


def settle_kernel(p0, a, b, keep, send):
    for out, start in ((send, ROWS), (keep, 0)):
        rows = slice(start, start + ROWS)
        total = p0[rows, :].astype(f32) + a[rows, :].astype(f32) + b[rows, :].astype(f32)
        out[...] = total.astype(bf16)


def settle(p0, a, b):
    shape = jax.ShapeDtypeStruct((ROWS, p0.shape[1]), bf16)
    return call(settle_kernel, (shape, shape), 8, in_specs=[VM] * 3, out_specs=[VM] * 2)(p0, a, b)


def finish_kernel(k0, k1, g0, g1, out, joined):
    c = lax.axis_index("row") % 2
    mine = pl.multiple_of(c * (3 * W), W)
    other = pl.multiple_of((1 - c) * (3 * W), W)
    for base, first, last in ((mine, k0, k1), (other, g0, g1)):
        joined[:, pl.ds(base, 2 * W)] = first[...]
        joined[:, pl.ds(pl.multiple_of(base + 2 * W, W), W)] = last[...]
    row = lax.broadcasted_iota(jnp.int32, (ROWS, ROWS), 0)
    col = lax.broadcasted_iota(jnp.int32, (ROWS, ROWS), 1)
    order = (col == row % BS * TROWS + row // BS).astype(f32).astype(bf16)
    out[...] = jnp.dot(order, joined[...], preferred_element_type=f32).astype(bf16)


def finish(kept, got):
    return call(
        finish_kernel,
        jax.ShapeDtypeStruct((ROWS, 6 * W), bf16),
        16,
        in_specs=[VM] * 4,
        out_specs=VM,
        scratch_shapes=[pltpu.VMEM((ROWS, 6 * W), bf16)],
    )(*kept, *got)


def body(
    orbitals,
    fock_blocks,
    fock_where,
    density_blocks,
    integrals,
    quartet_density,
    quartet_target,
    quartet_count,
):
    with jax.named_scope("fock"):
        fock = pack(fock_blocks, fock_where)
    with jax.named_scope("density"):
        ask_above = shift_row(quartet_density, -1)
        ask_below = shift_row(quartet_density, 1)
        pair = jnp.concatenate([density_blocks, swap_yh(density_blocks)], axis=0)
        moved0 = turned(orbitals, 0, (pair, ask_above, ask_below))
        pool = (pair, shift_z(pair, 1), shift_z(pair, -1), shift_z(pair, 2))
        own, for_above, for_below = select((quartet_density, ask_above, ask_below), pool)
        vectors = (own, shift_row(for_above, 1), shift_row(for_below, -1))
    with jax.named_scope("gather"):
        slots0 = join(*moved0, vectors[1:])
        left0, right0 = shift_x(slots0, 1), shift_x(slots0, -1)
        term = exchange(quartet_count, quartet_target, vectors, integrals)
        slots1 = join(*turned(orbitals, 1, (*vectors[1:], fock)), (term,))
        left1, right1 = shift_x(slots1, 1), shift_x(slots1, -1)
        far0, far1 = shift_x(left0, 1), shift_x(hold(right1, (left1,)), -1)
    with jax.named_scope("terms"):
        term = jnp.concatenate([term, swap_core(term)], axis=0)
        term = jnp.concatenate([term, swap_z(term, 1)], axis=0)
        term = hold(term, (slots1, left0, right0))
        term = jnp.concatenate([term, swap_yh(term)], axis=0)
    with jax.named_scope("fock"):
        fock_h = swap_yh(hold(fock, (term,)))
    with jax.named_scope("terms"):
        term = hold(term, (left1, right1))
        terms = (term, swap_z(term, 2))
    with jax.named_scope("fock"):
        near = tiles(True, (fock, swap_core(fock)), terms, ())
        fock_h = hold(fock_h, (near, far0, far1))
        far = tiles(False, (fock_h, swap_core(fock_h)), terms, ())
        mats = (near, far)
    with jax.named_scope("gather"):
        slots2 = join(*turned(orbitals, 2, terms[1:]), (far0, far1, far))
        left2, right2 = shift_x(slots2, 1), shift_x(slots2, -1)
    kept, got, mixed = [], [], ()
    for n in (2, 1):
        if n == 2:
            chunks = ((slots0, left0, right0, far0), (slots1, left1, right1, far1))
        else:
            with jax.named_scope("gather"):
                far2a = shift_x(hold(left2[:COLS], mixed), 1)
                far2b = shift_x(hold(right2[COLS:], mixed), -1)
            chunks = ((slots2, left2, right2, far2a, far2b),)
        with jax.named_scope("reduce"):
            (p2,) = product(mats, chunks, (2,), mixed)
            above, below = shift_z(p2[:ROWS], 1), shift_z(p2[ROWS:], -1)
            pp, pm = product(mats, chunks, (1, 3), tuple(kept), 20)
            pp, pm = merge(pp, pm, above, below, (left2, right2))
            mixed = (pp, pm)
            (p0,) = product(mats, chunks, (0,), mixed, 20)
            keep, send = settle(p0, shift_z(pp, 1), shift_z(pm, -1))
            kept.append(keep)
            got.append(swap_core(send))
    with jax.named_scope("finish"):
        return finish(kept, got)


def solution(mesh):
    return jax.shard_map(
        body,
        mesh=mesh,
        in_specs=(
            P("col", "row"),
            P(("row", "col"), None),
            P(("row", "col")),
            P(("row", "col"), None),
            P(("row", "col"), None, None),
            P(("row", "col")),
            P(("row", "col")),
            P(("row", "col")),
        ),
        out_specs=P("row", "col"),
        check_vma=False,
    )
```

```python
import functools

import jax
import jax.numpy as jnp
from jax import lax
from jax.experimental import pallas as pl
from jax.experimental.pallas import tpu as pltpu
from jax.sharding import PartitionSpec as P

BS = 32
TROWS, TCOLS = 24, 48
KCAP, PCAP, QCAP = 512, 40, 8
ROWS, COLS = TROWS * BS, TCOLS * BS
GROUPS = TCOLS // 4
EXT = 1024 + 128
W = 128
AXES = ("row", "col")
SLOT_A, SLOT_B = (1, 3, 0, 2), (0, 2, 1, 3)
MB = 1 << 20
bf16, f32 = jnp.bfloat16, jnp.float32


def coords(d):
    r, k = d // 8, d % 8
    return dict(x=r // 4, yl=r // 2 % 2, c=r % 2, z=k // 2, yh=k % 2)


def number(x, yl, c, z, yh):
    return ((x % 4) * 4 + yl * 2 + c) * 8 + (z % 4) * 2 + yh


def move(value, to):
    pairs = []
    for d in range(128):
        place = coords(d)
        target = dict(place)
        target.update(to(**place))
        pairs.append((d, number(**target)))
    return lax.ppermute(value, AXES, pairs)


def shift_x(value, by):
    return move(value, lambda x, **o: dict(x=x + by))


def shift_z(value, by):
    return move(value, lambda z, **o: dict(z=z + by))


def swap_z(value, by):
    return move(value, lambda z, **o: dict(z=z ^ by))


def swap_core(value):
    return move(value, lambda c, **o: dict(c=1 - c))


def swap_yh(value):
    return move(value, lambda yh, **o: dict(yh=1 - yh))


def shift_row(value, by):
    pairs = [(d, (d + 8 * by) % 128) for d in range(128)]
    return lax.ppermute(value, AXES, pairs)


def move_y(value, table):
    def to(yl, yh, **o):
        y = table[yh * 2 + yl]
        return dict(yl=y % 2, yh=y // 2)

    return move(value, to)


def here():
    r, k = lax.axis_index("row"), lax.axis_index("col")
    return dict(r=r, k=k, x=r // 4, yl=r // 2 % 2, c=r % 2, z=k // 2, yh=k % 2)


def call(kernel, out_shape, vmem, *, in_specs, after=(), gflop=0, **kw):
    n = len(after)
    run = pl.pallas_call(
        lambda *refs: kernel(*refs[n:]),
        out_shape=out_shape,
        in_specs=[ANY] * n + list(in_specs),
        compiler_params=pltpu.CompilerParams(vmem_limit_bytes=vmem * MB),
        cost_estimate=pl.CostEstimate(flops=gflop * 10**9 + 1, bytes_accessed=1, transcendentals=0),
        **kw,
    )
    return lambda *operands: run(*after, *operands)


VM = pl.BlockSpec(memory_space=pltpu.VMEM)
SM = pl.BlockSpec(memory_space=pltpu.SMEM)
ANY = pl.BlockSpec(memory_space=pl.ANY)


def select_kernel(req_own, req_a, req_b, p0, p1, p2, p3, out_own, out_a, out_b):
    at = here()
    parts = (p0, p1, p2, p3)
    steps = (0, 3, 1, 2)
    span = 2 * PCAP
    lane = lax.broadcasted_iota(jnp.int32, (16, span), 1)
    row = lax.broadcasted_iota(jnp.int32, (16, span), 0)
    for req, out in ((req_own, out_own), (req_a, out_a), (req_b, out_b)):
        want = jnp.full((16, span), -1, jnp.int32)
        for q in range(QCAP):
            want = jnp.where(row == q, req[q], want)
        total = jnp.zeros((16, 1024), f32)
        for part, step in zip(parts, steps):
            z = (at["z"] + step) % 4
            yh = jnp.where(lane < PCAP, at["yh"], 1 - at["yh"])
            held = (at["r"] * 8 + z * 2 + yh) * PCAP + jnp.where(lane < PCAP, lane, lane - PCAP)
            hot = (want == held).astype(f32).astype(bf16)
            total = total + jnp.dot(hot, part[...], preferred_element_type=f32)
        out[...] = total.astype(bf16)


def select(requests, parts):
    shape = jax.ShapeDtypeStruct((16, 1024), bf16)
    return call(
        select_kernel,
        (shape,) * 3,
        6,
        in_specs=[SM] * 3 + [VM] * 4,
        out_specs=[VM] * 3,
    )(*requests, *parts)


def terms_kernel(count, target, v0, v1, v2, integral, out, buf, sems):
    def fetch(q):
        return pltpu.make_async_copy(integral.at[q], buf.at[q], sems.at[q])

    for q in range(QCAP):
        fetch(q).start()
    out[...] = jnp.zeros_like(out)
    col = lax.broadcasted_iota(jnp.int32, (QCAP, 128), 1)
    row = lax.broadcasted_iota(jnp.int32, (QCAP, 128), 0)
    mark = jnp.zeros((QCAP, 128), jnp.int32)
    core = here()["c"]
    for i in range(QCAP):
        t = target[i]
        note = jnp.where(col == 0, t // KCAP, jnp.where(col == 1, t % KCAP // 32, jnp.where(col == 2, t % 32, core)))
        mark = jnp.where(row == i, note, mark)
    out[:, 1024:EXT] = mark.astype(f32).astype(bf16)
    v = v0[...].astype(f32) + v1[...].astype(f32) + v2[...].astype(f32)
    rows = lax.broadcasted_iota(jnp.int32, (16, 1024), 0)
    places = lax.broadcasted_iota(jnp.int32, (QCAP, 1024), 0)

    def one(q, carry):
        fetch(q).wait()
        vector = jnp.sum(jnp.where(rows == q, v, 0.0), axis=0, keepdims=True)
        sums = []
        for h in range(2):
            acc = jnp.zeros((512, 128), f32)
            for a in range(8):
                lanes = slice(a * 128, (a + 1) * 128)
                acc = acc + buf[q, h * 512 : (h + 1) * 512, lanes].astype(f32) * vector[:, lanes]
            sums.append(jnp.sum(acc.T, axis=0, keepdims=True))
        term = jnp.where(q < count[0], jnp.concatenate(sums, axis=1), 0.0)
        out[:, 0:1024] = jnp.where(places == q, term, out[:, 0:1024].astype(f32)).astype(bf16)
        return carry

    lax.fori_loop(0, QCAP, one, 0)


def exchange(count, target, vectors, integrals):
    return call(
        terms_kernel,
        jax.ShapeDtypeStruct((QCAP, EXT), bf16),
        48,
        in_specs=[SM, SM, VM, VM, VM, ANY],
        out_specs=VM,
        scratch_shapes=[pltpu.VMEM((QCAP, 1024, 1024), bf16), pltpu.SemaphoreType.DMA((QCAP,))],
    )(count, target, *vectors, integrals)


def tiles_kernel(near, f0, f1, t0, t1, out, f, tcur, wide, spread):
    g = pl.program_id(0)
    at = here()
    for i, stored in enumerate((f0, f1)):

        @pl.when(g == i)
        def _():
            f[...] = stored[...]

    @pl.when(g == 0)
    def _():
        for i, t in enumerate((t0, t1)):
            tcur[64 * i : 64 * i + 64, :] = t[...]

    k = at["z"] * 2 + (at["yh"] if near else 1 - at["yh"])
    marks = tcur[:, 1024:EXT].astype(f32)
    slot = (marks[:, 1:2] * 32.0 + marks[:, 2:3]).astype(jnp.int32)
    core = jnp.where(g == 0, at["c"], 1 - at["c"])
    slot = jnp.where(marks[:, 0:1].astype(jnp.int32) == k, slot, -1)
    slot = jnp.where(marks[:, 3:4].astype(jnp.int32) == core, slot, -1)
    spots = lax.broadcasted_iota(jnp.int32, (128, KCAP), 1)
    hot = (slot == spots).astype(f32).astype(bf16)
    update = lax.dot_general(hot, tcur[:, 0:1024], (((0,), (0,)), ((), ())), preferred_element_type=f32)
    fock = (f[:KCAP, :].astype(f32) + 0.25 * update).astype(bf16)
    place = f[KCAP:, :KCAP].astype(f32).T
    tr = place[:, 0:1].astype(jnp.int32)
    tc = place[:, 1:2].astype(jnp.int32)
    lane = lax.broadcasted_iota(jnp.int32, (KCAP, 512), 1)
    keep = (lane % 128 // BS) == (tc % 4)
    src = lax.broadcasted_iota(jnp.int32, (128, 512), 0)
    dst = lax.broadcasted_iota(jnp.int32, (128, 512), 1)
    copy = (src == dst // 128 * BS + dst % BS).astype(f32).astype(bf16)
    for a in range(8):
        piece = jnp.dot(fock[:, a * 128 : (a + 1) * 128], copy, preferred_element_type=f32)
        wide[:, a * 512 : (a + 1) * 512] = jnp.where(keep, piece, 0.0).astype(bf16)
    spot = lax.broadcasted_iota(jnp.int32, (KCAP, GROUPS * TROWS), 1)
    put = (spot == tc // 4 * TROWS + tr).astype(f32).astype(bf16)
    for h in range(8):
        spread[...] = lax.dot_general(
            put, wide[:, h * 512 : (h + 1) * 512], (((0,), (0,)), ((), ())), preferred_element_type=f32
        )
        for p in range(2):
            for t in range(GROUPS):
                pair = [
                    spread[t * TROWS : (t + 1) * TROWS, (2 * p + o) * 128 : (2 * p + o + 1) * 128]
                    for o in range(2)
                ]
                start = (4 * h + 2 * p) * TROWS
                out[start : start + 2 * TROWS, t * 128 : (t + 1) * 128] = jnp.concatenate(pair, axis=0).astype(bf16)


def tiles(near, focks, terms, after, gflop=0):
    return call(
        functools.partial(tiles_kernel, near),
        jax.ShapeDtypeStruct((2 * ROWS, COLS), bf16),
        24,
        after=after,
        gflop=gflop,
        grid=(2,),
        in_specs=[VM] * 4,
        out_specs=pl.BlockSpec((ROWS, COLS), lambda g: (g, 0)),
        scratch_shapes=[
            pltpu.VMEM((KCAP + 16, 1024), bf16),
            pltpu.VMEM((128, EXT), bf16),
            pltpu.VMEM((KCAP, 4096), bf16),
            pltpu.VMEM((GROUPS * TROWS, 512), f32),
        ],
    )(*focks, *terms)


def pack_kernel(blocks, where, out):
    out[:KCAP, :] = blocks[...]
    spot = jnp.concatenate([where[j : j + 1, :] for j in range(KCAP // 128)], axis=1)
    row = lax.broadcasted_iota(jnp.int32, (16, KCAP), 0)
    note = jnp.where(row == 0, spot // TCOLS, jnp.where(row == 1, spot % TCOLS, 0))
    out[KCAP:, :KCAP] = note.astype(f32).astype(bf16)
    out[KCAP:, KCAP:] = jnp.zeros((16, 1024 - KCAP), bf16)


def pack(blocks, where):
    return call(
        pack_kernel,
        jax.ShapeDtypeStruct((KCAP + 16, 1024), bf16),
        8,
        in_specs=[VM] * 2,
        out_specs=VM,
    )(blocks, where.reshape(KCAP // 128, 128))


def hold_kernel(start, value, out, sem):
    copy = pltpu.make_async_copy(value.at[start : start + out.shape[0]], out, sem)
    copy.start()
    copy.wait()


def hold(value, after, start=0, rows=None):
    return call(
        functools.partial(hold_kernel, start),
        jax.ShapeDtypeStruct((rows or value.shape[0], *value.shape[1:]), value.dtype),
        2,
        after=after,
        in_specs=[ANY],
        out_specs=ANY,
        scratch_shapes=[pltpu.SemaphoreType.DMA],
    )(value)


def cut_kernel(j, value, out, sem):
    copy = pltpu.make_async_copy(value.at[:, j * W : (j + 1) * W], out, sem)
    copy.start()
    copy.wait()


def cut(value, j, after):
    return call(
        functools.partial(cut_kernel, j),
        jax.ShapeDtypeStruct((COLS, W), bf16),
        2,
        after=after,
        in_specs=[ANY],
        out_specs=ANY,
        scratch_shapes=[pltpu.SemaphoreType.DMA],
    )(value)


def join_kernel(a, b, out, sems):
    copies = [pltpu.make_async_copy(src, out.at[i * COLS : (i + 1) * COLS], sems.at[i]) for i, src in enumerate((a, b))]
    for copy in copies:
        copy.start()
    for copy in copies:
        copy.wait()


def join(a, b, after):
    return call(
        join_kernel,
        jax.ShapeDtypeStruct((2 * COLS, W), bf16),
        2,
        after=after,
        in_specs=[ANY] * 2,
        out_specs=ANY,
        scratch_shapes=[pltpu.SemaphoreType.DMA((2,))],
    )(a, b)


def turned(orbitals, j, after):
    piece = cut(orbitals, j, after)
    return move_y(piece, SLOT_A), move_y(piece, SLOT_B)


def product_kernel(sizes, steps, near, far, *refs):
    at = here()
    n = len(sizes)
    wide = n * W
    blocks, outs, cols, sems = refs[: sum(sizes)], refs[sum(sizes) : -2], refs[-2], refs[-1]
    first = jnp.where(at["yh"] == at["yl"], COLS, 0)
    copies = []
    base = 0
    for j, size in enumerate(sizes):
        plan = [(b, s, h, h * COLS) for b, s in ((0, 0), (1, 3), (2, 1)) for h in range(2)]
        if size == 4:
            plan += [(3, 2, 0, 0), (3, 2, 1, COLS)]
        else:
            plan += [(3, 2, 0, 0), (4, 2, 1, 0)]
        for b, step, slot, start in plan:
            to = (at["x"] + step - at["z"] + 4) % 4
            wanted, place = to == steps[0], 0
            for i, other in enumerate(steps[1:]):
                wanted = jnp.logical_or(wanted, to == other)
                place = jnp.where(to == other, i + 1, place)
            lane = pl.multiple_of((place * n + j) * W, W)
            row = pl.multiple_of(first if slot == 0 else COLS - first, COLS)
            dst = cols.at[pl.ds(row, COLS), pl.ds(lane, W)]
            copy = pltpu.make_async_copy(blocks[base + b].at[start : start + COLS], dst, sems.at[len(copies)])
            copies.append((wanted, copy))
        base += size
    for wanted, copy in copies:

        @pl.when(wanted)
        def _():
            copy.start()

    for wanted, copy in copies:

        @pl.when(wanted)
        def _():
            copy.wait()

    for i in range(2):
        rows = slice(i * ROWS, (i + 1) * ROWS)
        part = jnp.dot(near[rows, :], cols[:COLS, :], preferred_element_type=f32)
        part = (part + jnp.dot(far[rows, :], cols[COLS:, :], preferred_element_type=f32)).astype(bf16)
        for o, out in enumerate(outs):
            out[rows, :] = part[:, o * wide : (o + 1) * wide]


def product(mats, chunks, steps, after=(), gflop=0):
    n = len(chunks)
    sizes = tuple(len(c) for c in chunks)
    return call(
        functools.partial(product_kernel, sizes, steps),
        (jax.ShapeDtypeStruct((2 * ROWS, n * W), bf16),) * len(steps),
        24,
        after=after,
        gflop=gflop,
        in_specs=[VM] * 2 + [ANY] * sum(sizes),
        out_specs=[VM] * len(steps),
        scratch_shapes=[pltpu.VMEM((2 * COLS, len(steps) * n * W), bf16), pltpu.SemaphoreType.DMA((8 * n,))],
    )(*mats, *(b for c in chunks for b in c))


def merge_kernel(pp, pm, above, below, pp_out, pm_out):
    pp_out[:ROWS, :] = (pp[:ROWS, :].astype(f32) + above[...].astype(f32)).astype(bf16)
    pp_out[ROWS:, :] = pp[ROWS:, :]
    pm_out[:ROWS, :] = pm[:ROWS, :]
    pm_out[ROWS:, :] = (pm[ROWS:, :].astype(f32) + below[...].astype(f32)).astype(bf16)


def merge(pp, pm, above, below, after):
    shape = jax.ShapeDtypeStruct(pp.shape, bf16)
    return call(merge_kernel, (shape, shape), 8, after=after, in_specs=[VM] * 4, out_specs=[VM] * 2)(
        pp, pm, above, below
    )


def settle_kernel(p0, a, b, keep, send):
    for out, start in ((send, ROWS), (keep, 0)):
        rows = slice(start, start + ROWS)
        total = p0[rows, :].astype(f32) + a[rows, :].astype(f32) + b[rows, :].astype(f32)
        out[...] = total.astype(bf16)


def settle(p0, a, b):
    shape = jax.ShapeDtypeStruct((ROWS, p0.shape[1]), bf16)
    return call(settle_kernel, (shape, shape), 8, in_specs=[VM] * 3, out_specs=[VM] * 2)(p0, a, b)


def finish_kernel(k0, k1, g0, g1, out, joined):
    c = lax.axis_index("row") % 2
    mine = pl.multiple_of(c * (3 * W), W)
    other = pl.multiple_of((1 - c) * (3 * W), W)
    for base, first, last in ((mine, k0, k1), (other, g0, g1)):
        joined[:, pl.ds(base, 2 * W)] = first[...]
        joined[:, pl.ds(pl.multiple_of(base + 2 * W, W), W)] = last[...]
    row = lax.broadcasted_iota(jnp.int32, (ROWS, ROWS), 0)
    col = lax.broadcasted_iota(jnp.int32, (ROWS, ROWS), 1)
    order = (col == row % BS * TROWS + row // BS).astype(f32).astype(bf16)
    out[...] = jnp.dot(order, joined[...], preferred_element_type=f32).astype(bf16)


def finish(kept, got):
    return call(
        finish_kernel,
        jax.ShapeDtypeStruct((ROWS, 6 * W), bf16),
        16,
        in_specs=[VM] * 4,
        out_specs=VM,
        scratch_shapes=[pltpu.VMEM((ROWS, 6 * W), bf16)],
    )(*kept, *got)


def body(
    orbitals,
    fock_blocks,
    fock_where,
    density_blocks,
    integrals,
    quartet_density,
    quartet_target,
    quartet_count,
):
    with jax.named_scope("fock"):
        fock = pack(fock_blocks, fock_where)
    with jax.named_scope("density"):
        ask_above = shift_row(quartet_density, -1)
        ask_below = shift_row(quartet_density, 1)
        pair = jnp.concatenate([density_blocks, swap_yh(density_blocks)], axis=0)
        piece0 = hold(orbitals[:, :W], (pair, ask_above, ask_below))
        moved0 = (move_y(piece0, SLOT_A), move_y(piece0, SLOT_B))
        pool = (pair, shift_z(pair, 1), shift_z(pair, -1), shift_z(pair, 2))
        own, for_above, for_below = select((quartet_density, ask_above, ask_below), pool)
        vectors = (own, shift_row(for_above, 1), shift_row(for_below, -1))
    with jax.named_scope("gather"):
        slots0 = join(*moved0, vectors[1:])
        left0, right0 = shift_x(slots0, 1), shift_x(slots0, -1)
        term = exchange(quartet_count, quartet_target, vectors, integrals)
        slots1 = join(*turned(orbitals, 1, (*vectors[1:], fock)), (term,))
        left1, right1 = shift_x(slots1, 1), shift_x(slots1, -1)
        far0, far1 = shift_x(left0, 1), shift_x(hold(right1, (left1,)), -1)
    with jax.named_scope("terms"):
        term = jnp.concatenate([term, swap_core(term)], axis=0)
        term = jnp.concatenate([term, swap_z(term, 1)], axis=0)
        term = hold(term, (slots1, left0, right0))
        term = jnp.concatenate([term, swap_yh(term)], axis=0)
    with jax.named_scope("fock"):
        fock_h = swap_yh(hold(fock, (term,)))
    with jax.named_scope("terms"):
        term = hold(term, (left1, right1))
        terms = (term, swap_z(term, 2))
    with jax.named_scope("fock"):
        near = tiles(True, (fock, swap_core(fock)), terms, ())
        fock_h = hold(fock_h, (near, far0, far1))
        far = tiles(False, (fock_h, swap_core(fock_h)), terms, ())
        mats = (near, far)
    with jax.named_scope("gather"):
        slots2 = join(*turned(orbitals, 2, terms[1:]), (far0, far1, far))
        left2, right2 = shift_x(slots2, 1), shift_x(slots2, -1)
    kept, got, mixed = [], [], ()
    for n in (2, 1):
        if n == 2:
            chunks = ((slots0, left0, right0, far0), (slots1, left1, right1, far1))
        else:
            with jax.named_scope("gather"):
                far2a = shift_x(hold(left2[:COLS], mixed), 1)
                far2b = shift_x(hold(right2[COLS:], mixed), -1)
            chunks = ((slots2, left2, right2, far2a, far2b),)
        with jax.named_scope("reduce"):
            (p2,) = product(mats, chunks, (2,), mixed)
            above, below = shift_z(p2[:ROWS], 1), shift_z(p2[ROWS:], -1)
            pp, pm = product(mats, chunks, (1, 3), tuple(kept), 20)
            pp, pm = merge(pp, pm, above, below, (left2, right2))
            mixed = (pp, pm)
            (p0,) = product(mats, chunks, (0,), mixed, 20)
            keep, send = settle(p0, shift_z(pp, 1), shift_z(pm, -1))
            kept.append(keep)
            got.append(swap_core(send))
    with jax.named_scope("finish"):
        return finish(kept, got)


def solution(mesh):
    return jax.shard_map(
        body,
        mesh=mesh,
        in_specs=(
            P("col", "row"),
            P(("row", "col"), None),
            P(("row", "col")),
            P(("row", "col"), None),
            P(("row", "col"), None, None),
            P(("row", "col")),
            P(("row", "col")),
            P(("row", "col")),
        ),
        out_specs=P("row", "col"),
        check_vma=False,
    )
```

```python
import functools

import jax
import jax.numpy as jnp
from jax import lax
from jax.experimental import pallas as pl
from jax.experimental.pallas import tpu as pltpu
from jax.sharding import PartitionSpec as P

BS = 32
TROWS, TCOLS = 24, 48
KCAP, PCAP, QCAP = 512, 40, 8
ROWS, COLS = TROWS * BS, TCOLS * BS
GROUPS = TCOLS // 4
EXT = 1024 + 128
W = 128
AXES = ("row", "col")
SLOT_A, SLOT_B = (1, 3, 0, 2), (0, 2, 1, 3)
MB = 1 << 20
bf16, f32 = jnp.bfloat16, jnp.float32


def coords(d):
    r, k = d // 8, d % 8
    return dict(x=r // 4, yl=r // 2 % 2, c=r % 2, z=k // 2, yh=k % 2)


def number(x, yl, c, z, yh):
    return ((x % 4) * 4 + yl * 2 + c) * 8 + (z % 4) * 2 + yh


def move(value, to):
    pairs = []
    for d in range(128):
        place = coords(d)
        target = dict(place)
        target.update(to(**place))
        pairs.append((d, number(**target)))
    return lax.ppermute(value, AXES, pairs)


def shift_x(value, by):
    return move(value, lambda x, **o: dict(x=x + by))


def shift_z(value, by):
    return move(value, lambda z, **o: dict(z=z + by))


def swap_z(value, by):
    return move(value, lambda z, **o: dict(z=z ^ by))


def swap_core(value):
    return move(value, lambda c, **o: dict(c=1 - c))


def swap_yh(value):
    return move(value, lambda yh, **o: dict(yh=1 - yh))


def shift_row(value, by):
    pairs = [(d, (d + 8 * by) % 128) for d in range(128)]
    return lax.ppermute(value, AXES, pairs)


def move_y(value, table):
    def to(yl, yh, **o):
        y = table[yh * 2 + yl]
        return dict(yl=y % 2, yh=y // 2)

    return move(value, to)


def here():
    r, k = lax.axis_index("row"), lax.axis_index("col")
    return dict(r=r, k=k, x=r // 4, yl=r // 2 % 2, c=r % 2, z=k // 2, yh=k % 2)


def call(kernel, out_shape, vmem, *, in_specs, after=(), gflop=0, **kw):
    n = len(after)
    run = pl.pallas_call(
        lambda *refs: kernel(*refs[n:]),
        out_shape=out_shape,
        in_specs=[ANY] * n + list(in_specs),
        compiler_params=pltpu.CompilerParams(vmem_limit_bytes=vmem * MB),
        cost_estimate=pl.CostEstimate(flops=gflop * 10**9 + 1, bytes_accessed=1, transcendentals=0),
        **kw,
    )
    return lambda *operands: run(*after, *operands)


VM = pl.BlockSpec(memory_space=pltpu.VMEM)
SM = pl.BlockSpec(memory_space=pltpu.SMEM)
ANY = pl.BlockSpec(memory_space=pl.ANY)


def select_kernel(req_own, req_a, req_b, p0, p1, p2, p3, out_own, out_a, out_b):
    at = here()
    parts = (p0, p1, p2, p3)
    steps = (0, 3, 1, 2)
    span = 2 * PCAP
    lane = lax.broadcasted_iota(jnp.int32, (16, span), 1)
    row = lax.broadcasted_iota(jnp.int32, (16, span), 0)
    for req, out in ((req_own, out_own), (req_a, out_a), (req_b, out_b)):
        want = jnp.full((16, span), -1, jnp.int32)
        for q in range(QCAP):
            want = jnp.where(row == q, req[q], want)
        total = jnp.zeros((16, 1024), f32)
        for part, step in zip(parts, steps):
            z = (at["z"] + step) % 4
            yh = jnp.where(lane < PCAP, at["yh"], 1 - at["yh"])
            held = (at["r"] * 8 + z * 2 + yh) * PCAP + jnp.where(lane < PCAP, lane, lane - PCAP)
            hot = (want == held).astype(f32).astype(bf16)
            total = total + jnp.dot(hot, part[...], preferred_element_type=f32)
        out[...] = total.astype(bf16)


def select(requests, parts):
    shape = jax.ShapeDtypeStruct((16, 1024), bf16)
    return call(
        select_kernel,
        (shape,) * 3,
        6,
        in_specs=[SM] * 3 + [VM] * 4,
        out_specs=[VM] * 3,
    )(*requests, *parts)


def terms_kernel(count, target, v0, v1, v2, integral, out, buf, sems):
    def fetch(q):
        return pltpu.make_async_copy(integral.at[q], buf.at[q], sems.at[q])

    for q in range(QCAP):
        fetch(q).start()
    out[...] = jnp.zeros_like(out)
    col = lax.broadcasted_iota(jnp.int32, (QCAP, 128), 1)
    row = lax.broadcasted_iota(jnp.int32, (QCAP, 128), 0)
    mark = jnp.zeros((QCAP, 128), jnp.int32)
    core = here()["c"]
    for i in range(QCAP):
        t = target[i]
        note = jnp.where(col == 0, t // KCAP, jnp.where(col == 1, t % KCAP // 32, jnp.where(col == 2, t % 32, core)))
        mark = jnp.where(row == i, note, mark)
    out[:, 1024:EXT] = mark.astype(f32).astype(bf16)
    v = v0[...].astype(f32) + v1[...].astype(f32) + v2[...].astype(f32)
    rows = lax.broadcasted_iota(jnp.int32, (16, 1024), 0)
    places = lax.broadcasted_iota(jnp.int32, (QCAP, 1024), 0)

    def one(q, carry):
        fetch(q).wait()
        vector = jnp.sum(jnp.where(rows == q, v, 0.0), axis=0, keepdims=True)
        sums = []
        for h in range(2):
            acc = jnp.zeros((512, 128), f32)
            for a in range(8):
                lanes = slice(a * 128, (a + 1) * 128)
                acc = acc + buf[q, h * 512 : (h + 1) * 512, lanes].astype(f32) * vector[:, lanes]
            sums.append(jnp.sum(acc.T, axis=0, keepdims=True))
        term = jnp.where(q < count[0], jnp.concatenate(sums, axis=1), 0.0)
        out[:, 0:1024] = jnp.where(places == q, term, out[:, 0:1024].astype(f32)).astype(bf16)
        return carry

    lax.fori_loop(0, QCAP, one, 0)


def exchange(count, target, vectors, integrals):
    return call(
        terms_kernel,
        jax.ShapeDtypeStruct((QCAP, EXT), bf16),
        48,
        in_specs=[SM, SM, VM, VM, VM, ANY],
        out_specs=VM,
        scratch_shapes=[pltpu.VMEM((QCAP, 1024, 1024), bf16), pltpu.SemaphoreType.DMA((QCAP,))],
    )(count, target, *vectors, integrals)


def tiles_kernel(near, f0, f1, t0, t1, out, f, tcur):
    g = pl.program_id(0)
    at = here()
    for i, stored in enumerate((f0, f1)):

        @pl.when(g == i)
        def _():
            f[...] = stored[...]

    @pl.when(g == 0)
    def _():
        for i, t in enumerate((t0, t1)):
            tcur[64 * i : 64 * i + 64, :] = t[...]

    k = at["z"] * 2 + (at["yh"] if near else 1 - at["yh"])
    marks = tcur[:, 1024:EXT].astype(f32)
    slot = (marks[:, 1:2] * 32.0 + marks[:, 2:3]).astype(jnp.int32)
    core = jnp.where(g == 0, at["c"], 1 - at["c"])
    slot = jnp.where(marks[:, 0:1].astype(jnp.int32) == k, slot, -1)
    slot = jnp.where(marks[:, 3:4].astype(jnp.int32) == core, slot, -1)
    spots = lax.broadcasted_iota(jnp.int32, (128, KCAP), 1)
    hot = (slot == spots).astype(f32).astype(bf16)
    update = lax.dot_general(hot, tcur[:, 0:1024], (((0,), (0,)), ((), ())), preferred_element_type=f32)
    fock = (f[:KCAP, :].astype(f32) + 0.25 * update).astype(bf16)
    place = f[KCAP:, :KCAP].astype(f32).T
    tr = place[:, 0:1].astype(jnp.int32)
    tc = place[:, 1:2].astype(jnp.int32)
    lane = lax.broadcasted_iota(jnp.int32, (KCAP, 512), 1)
    keep = (lane % 128 // BS) == (tc % 4)
    src = lax.broadcasted_iota(jnp.int32, (128, 512), 0)
    dst = lax.broadcasted_iota(jnp.int32, (128, 512), 1)
    copy = (src == dst // 128 * BS + dst % BS).astype(f32).astype(bf16)
    spot = lax.broadcasted_iota(jnp.int32, (KCAP, GROUPS * TROWS), 1)
    put = (spot == tc // 4 * TROWS + tr).astype(f32).astype(bf16)
    for h in range(8):
        piece = jnp.dot(fock[:, h * 128 : (h + 1) * 128], copy, preferred_element_type=f32)
        wide = jnp.where(keep, piece, 0.0).astype(bf16)
        spread = lax.dot_general(put, wide, (((0,), (0,)), ((), ())), preferred_element_type=f32)
        for p in range(2):
            for t in range(GROUPS):
                pair = [
                    spread[t * TROWS : (t + 1) * TROWS, (2 * p + o) * 128 : (2 * p + o + 1) * 128]
                    for o in range(2)
                ]
                start = (4 * h + 2 * p) * TROWS
                out[start : start + 2 * TROWS, t * 128 : (t + 1) * 128] = jnp.concatenate(pair, axis=0).astype(bf16)


def tiles(near, focks, terms, after, gflop=0):
    return call(
        functools.partial(tiles_kernel, near),
        jax.ShapeDtypeStruct((2 * ROWS, COLS), bf16),
        24,
        after=after,
        gflop=gflop,
        grid=(2,),
        in_specs=[VM] * 4,
        out_specs=pl.BlockSpec((ROWS, COLS), lambda g: (g, 0)),
        scratch_shapes=[
            pltpu.VMEM((KCAP + 16, 1024), bf16),
            pltpu.VMEM((128, EXT), bf16),
        ],
    )(*focks, *terms)


def pack_kernel(blocks, where, out):
    out[:KCAP, :] = blocks[...]
    spot = jnp.concatenate([where[j : j + 1, :] for j in range(KCAP // 128)], axis=1)
    row = lax.broadcasted_iota(jnp.int32, (16, KCAP), 0)
    note = jnp.where(row == 0, spot // TCOLS, jnp.where(row == 1, spot % TCOLS, 0))
    out[KCAP:, :KCAP] = note.astype(f32).astype(bf16)
    out[KCAP:, KCAP:] = jnp.zeros((16, 1024 - KCAP), bf16)


def pack(blocks, where):
    return call(
        pack_kernel,
        jax.ShapeDtypeStruct((KCAP + 16, 1024), bf16),
        8,
        in_specs=[VM] * 2,
        out_specs=VM,
    )(blocks, where.reshape(KCAP // 128, 128))


def hold_kernel(start, value, out, sem):
    copy = pltpu.make_async_copy(value.at[start : start + out.shape[0]], out, sem)
    copy.start()
    copy.wait()


def hold(value, after, start=0, rows=None):
    return call(
        functools.partial(hold_kernel, start),
        jax.ShapeDtypeStruct((rows or value.shape[0], *value.shape[1:]), value.dtype),
        2,
        after=after,
        in_specs=[ANY],
        out_specs=ANY,
        scratch_shapes=[pltpu.SemaphoreType.DMA],
    )(value)


def cut_kernel(j, value, out, sem):
    copy = pltpu.make_async_copy(value.at[:, j * W : (j + 1) * W], out, sem)
    copy.start()
    copy.wait()


def cut(value, j, after):
    return call(
        functools.partial(cut_kernel, j),
        jax.ShapeDtypeStruct((COLS, W), bf16),
        2,
        after=after,
        in_specs=[ANY],
        out_specs=ANY,
        scratch_shapes=[pltpu.SemaphoreType.DMA],
    )(value)


def join_kernel(a, b, out, sems):
    copies = [pltpu.make_async_copy(src, out.at[i * COLS : (i + 1) * COLS], sems.at[i]) for i, src in enumerate((a, b))]
    for copy in copies:
        copy.start()
    for copy in copies:
        copy.wait()


def join(a, b, after):
    return call(
        join_kernel,
        jax.ShapeDtypeStruct((2 * COLS, W), bf16),
        2,
        after=after,
        in_specs=[ANY] * 2,
        out_specs=ANY,
        scratch_shapes=[pltpu.SemaphoreType.DMA((2,))],
    )(a, b)


def turned(orbitals, j, after):
    piece = cut(orbitals, j, after)
    return move_y(piece, SLOT_A), move_y(piece, SLOT_B)


def product_kernel(sizes, steps, near, far, *refs):
    at = here()
    n = len(sizes)
    wide = n * W
    blocks, outs, cols, sems = refs[: sum(sizes)], refs[sum(sizes) : -2], refs[-2], refs[-1]
    first = jnp.where(at["yh"] == at["yl"], COLS, 0)
    copies = []
    base = 0
    for j, size in enumerate(sizes):
        plan = [(b, s, h, h * COLS) for b, s in ((0, 0), (1, 3), (2, 1)) for h in range(2)]
        if size == 4:
            plan += [(3, 2, 0, 0), (3, 2, 1, COLS)]
        else:
            plan += [(3, 2, 0, 0), (4, 2, 1, 0)]
        for b, step, slot, start in plan:
            to = (at["x"] + step - at["z"] + 4) % 4
            wanted, place = to == steps[0], 0
            for i, other in enumerate(steps[1:]):
                wanted = jnp.logical_or(wanted, to == other)
                place = jnp.where(to == other, i + 1, place)
            lane = pl.multiple_of((place * n + j) * W, W)
            row = pl.multiple_of(first if slot == 0 else COLS - first, COLS)
            dst = cols.at[pl.ds(row, COLS), pl.ds(lane, W)]
            copy = pltpu.make_async_copy(blocks[base + b].at[start : start + COLS], dst, sems.at[len(copies)])
            copies.append((wanted, copy))
        base += size
    for wanted, copy in copies:

        @pl.when(wanted)
        def _():
            copy.start()

    for wanted, copy in copies:

        @pl.when(wanted)
        def _():
            copy.wait()

    for i in range(2):
        rows = slice(i * ROWS, (i + 1) * ROWS)
        part = jnp.dot(near[rows, :], cols[:COLS, :], preferred_element_type=f32)
        part = (part + jnp.dot(far[rows, :], cols[COLS:, :], preferred_element_type=f32)).astype(bf16)
        for o, out in enumerate(outs):
            out[rows, :] = part[:, o * wide : (o + 1) * wide]


def product(mats, chunks, steps, after=(), gflop=0):
    n = len(chunks)
    sizes = tuple(len(c) for c in chunks)
    return call(
        functools.partial(product_kernel, sizes, steps),
        (jax.ShapeDtypeStruct((2 * ROWS, n * W), bf16),) * len(steps),
        24,
        after=after,
        gflop=gflop,
        in_specs=[VM] * 2 + [ANY] * sum(sizes),
        out_specs=[VM] * len(steps),
        scratch_shapes=[pltpu.VMEM((2 * COLS, len(steps) * n * W), bf16), pltpu.SemaphoreType.DMA((8 * n,))],
    )(*mats, *(b for c in chunks for b in c))


def merge_kernel(pp, pm, above, below, pp_out, pm_out):
    pp_out[:ROWS, :] = (pp[:ROWS, :].astype(f32) + above[...].astype(f32)).astype(bf16)
    pp_out[ROWS:, :] = pp[ROWS:, :]
    pm_out[:ROWS, :] = pm[:ROWS, :]
    pm_out[ROWS:, :] = (pm[ROWS:, :].astype(f32) + below[...].astype(f32)).astype(bf16)


def merge(pp, pm, above, below, after):
    shape = jax.ShapeDtypeStruct(pp.shape, bf16)
    return call(merge_kernel, (shape, shape), 8, after=after, in_specs=[VM] * 4, out_specs=[VM] * 2)(
        pp, pm, above, below
    )


def settle_kernel(p0, a, b, keep, send):
    for out, start in ((send, ROWS), (keep, 0)):
        rows = slice(start, start + ROWS)
        total = p0[rows, :].astype(f32) + a[rows, :].astype(f32) + b[rows, :].astype(f32)
        out[...] = total.astype(bf16)


def settle(p0, a, b):
    shape = jax.ShapeDtypeStruct((ROWS, p0.shape[1]), bf16)
    return call(settle_kernel, (shape, shape), 8, in_specs=[VM] * 3, out_specs=[VM] * 2)(p0, a, b)


def finish_kernel(k0, k1, g0, g1, out, joined):
    c = lax.axis_index("row") % 2
    mine = pl.multiple_of(c * (3 * W), W)
    other = pl.multiple_of((1 - c) * (3 * W), W)
    for base, first, last in ((mine, k0, k1), (other, g0, g1)):
        joined[:, pl.ds(base, 2 * W)] = first[...]
        joined[:, pl.ds(pl.multiple_of(base + 2 * W, W), W)] = last[...]
    row = lax.broadcasted_iota(jnp.int32, (ROWS, ROWS), 0)
    col = lax.broadcasted_iota(jnp.int32, (ROWS, ROWS), 1)
    order = (col == row % BS * TROWS + row // BS).astype(f32).astype(bf16)
    out[...] = jnp.dot(order, joined[...], preferred_element_type=f32).astype(bf16)


def finish(kept, got):
    return call(
        finish_kernel,
        jax.ShapeDtypeStruct((ROWS, 6 * W), bf16),
        16,
        in_specs=[VM] * 4,
        out_specs=VM,
        scratch_shapes=[pltpu.VMEM((ROWS, 6 * W), bf16)],
    )(*kept, *got)


def body(
    orbitals,
    fock_blocks,
    fock_where,
    density_blocks,
    integrals,
    quartet_density,
    quartet_target,
    quartet_count,
):
    with jax.named_scope("fock"):
        fock = pack(fock_blocks, fock_where)
    with jax.named_scope("density"):
        ask_above = shift_row(quartet_density, -1)
        ask_below = shift_row(quartet_density, 1)
        pair = jnp.concatenate([density_blocks, swap_yh(density_blocks)], axis=0)
        piece0 = hold(orbitals[:, :W], (pair, ask_above, ask_below))
        moved0 = (move_y(piece0, SLOT_A), move_y(piece0, SLOT_B))
        pool = (pair, shift_z(pair, 1), shift_z(pair, -1), shift_z(pair, 2))
        own, for_above, for_below = select((quartet_density, ask_above, ask_below), pool)
        vectors = (own, shift_row(for_above, 1), shift_row(for_below, -1))
    with jax.named_scope("gather"):
        slots0 = join(*moved0, vectors[1:])
        left0, right0 = shift_x(slots0, 1), shift_x(slots0, -1)
        term = exchange(quartet_count, quartet_target, vectors, integrals)
        slots1 = join(*turned(orbitals, 1, (*vectors[1:], fock)), (term,))
        left1, right1 = shift_x(slots1, 1), shift_x(slots1, -1)
        far0, far1 = shift_x(left0, 1), shift_x(hold(right1, (left1,)), -1)
    with jax.named_scope("terms"):
        term = jnp.concatenate([term, swap_core(term)], axis=0)
        term = jnp.concatenate([term, swap_z(term, 1)], axis=0)
        term = hold(term, (slots1, left0, right0))
        term = jnp.concatenate([term, swap_yh(term)], axis=0)
    with jax.named_scope("fock"):
        fock_h = swap_yh(hold(fock, (term,)))
    with jax.named_scope("terms"):
        term = hold(term, (left1, right1))
        terms = (term, swap_z(term, 2))
    with jax.named_scope("fock"):
        near = tiles(True, (fock, swap_core(fock)), terms, ())
        fock_h = hold(fock_h, (near, far0, far1))
        far = tiles(False, (fock_h, swap_core(fock_h)), terms, ())
        mats = (near, far)
    with jax.named_scope("gather"):
        slots2 = join(*turned(orbitals, 2, terms[1:]), (far0, far1, far))
        left2, right2 = shift_x(slots2, 1), shift_x(slots2, -1)
    kept, got, mixed = [], [], ()
    for n in (2, 1):
        if n == 2:
            chunks = ((slots0, left0, right0, far0), (slots1, left1, right1, far1))
        else:
            with jax.named_scope("gather"):
                far2a = shift_x(hold(left2[:COLS], mixed), 1)
                far2b = shift_x(hold(right2[COLS:], mixed), -1)
            chunks = ((slots2, left2, right2, far2a, far2b),)
        with jax.named_scope("reduce"):
            (p2,) = product(mats, chunks, (2,), mixed)
            above, below = shift_z(p2[:ROWS], 1), shift_z(p2[ROWS:], -1)
            pp, pm = product(mats, chunks, (1, 3), tuple(kept), 20)
            pp, pm = merge(pp, pm, above, below, (left2, right2))
            mixed = (pp, pm)
            (p0,) = product(mats, chunks, (0,), mixed, 20)
            keep, send = settle(p0, shift_z(pp, 1), shift_z(pm, -1))
            kept.append(keep)
            got.append(swap_core(send))
    with jax.named_scope("finish"):
        return finish(kept, got)


def solution(mesh):
    return jax.shard_map(
        body,
        mesh=mesh,
        in_specs=(
            P("col", "row"),
            P(("row", "col"), None),
            P(("row", "col")),
            P(("row", "col"), None),
            P(("row", "col"), None, None),
            P(("row", "col")),
            P(("row", "col")),
            P(("row", "col")),
        ),
        out_specs=P("row", "col"),
        check_vma=False,
    )
```
